256 devices in a mesh: seq: 4 (over z_hi, core), res: 64 (over x, y, z_lo).
Axes of the slice: x: 4, y: 4, z: 8 (z_hi: 2, z_lo: 4; z = z_hi * 4 + z_lo), core: 2. Of those that a mesh axis runs over, the one named last changes fastest.
Arguments:
- homolog_activations: bfloat16 [1024, 768, 64], P('seq', 'res'), may hold values from -6 to 6
- present_entry_flags: int32 [1024, 768], P('seq', 'res'), may hold values from 0 to 1
- normalizer_scale: float32 [64], replicated, may hold values from 0.5 to 1.5
- normalizer_shift: float32 [64], replicated, may hold values from -1.5 to 1.5
- first_factor_weights: bfloat16 [64, 32], replicated, may hold values from -0.75 to 0.75
- first_factor_offset: float32 [32], replicated, may hold values from -0.9 to 0.9
- second_factor_weights: bfloat16 [64, 32], replicated, may hold values from -0.75 to 0.75
- second_factor_offset: float32 [32], replicated, may hold values from -0.9 to 0.9
- pairwise_readout_weights: bfloat16 [1024, 128], replicated, may hold values from -3 to 3
- pairwise_features: bfloat16 [768, 768, 128], P('res', 'seq'), may hold values from -3 to 3
Outputs:
- pair_out: bfloat16 [768, 768, 128], P('res', 'seq')
The draws below stay inside these ranges and needn't reach their ends.
All inputs are finite; a program needn't handle non-finite values.
Results may differ from the reference program's by a relative error of at most 0.0047.
Values may be sent and summed in bfloat16 or wider, within the bound.
A program may use at most 192 MiB of HBM per device.

```python
import jax
import jax.numpy as jnp
from jax import lax

FEATURE_DEPTH = 64
FACTOR_WIDTH = 32
CZ = 128
RES_DEV = 12
CHAIN_LENGTH = 768
HOMOLOG_COUNT = 1024


def draw_present_entry_flags(key, part):
    key = jax.random.fold_in(key, 11)
    keys = jax.random.split(key, 7)
    shortest = max(CHAIN_LENGTH // 4, 1)
    spans = jax.random.randint(keys[0], (HOMOLOG_COUNT, 1), shortest, CHAIN_LENGTH + 1)
    offsets = jax.random.randint(keys[1], (HOMOLOG_COUNT, 1), 0, 1 << 20) % (CHAIN_LENGTH - spans + 1)
    positions = jnp.arange(CHAIN_LENGTH, dtype=jnp.int32)[None, :]
    covered = (positions >= offsets) & (positions < offsets + spans)
    gap_width = jax.random.randint(keys[2], (HOMOLOG_COUNT, 1), 0, CHAIN_LENGTH // 8 + 1)
    gap_begin = offsets + jax.random.randint(keys[3], (HOMOLOG_COUNT, 1), 0, 1 << 20) % spans
    in_gap = (positions >= gap_begin) & (positions < gap_begin + gap_width)
    presence = jax.random.randint(keys[4], (HOMOLOG_COUNT, 1), 30, 101)
    coins = jax.random.randint(keys[5], (HOMOLOG_COUNT, CHAIN_LENGTH), 0, 100)
    kept = covered & jnp.logical_not(in_gap) & (coins < presence)
    ranking = jax.random.permutation(keys[6], HOMOLOG_COUNT)
    complete = (ranking < max(HOMOLOG_COUNT // 8, 1))[:, None]
    return jnp.where(complete, 1, kept.astype(jnp.int32)).astype(jnp.int32)


def steps_of(stream_key, shape, cuts, low, top_value):
    level = 1.0
    for axis_at, blocks in cuts:
        steps = jax.random.uniform(jax.random.fold_in(jax.random.fold_in(stream_key, 6), axis_at), (blocks,), jnp.float32, low / len(cuts), top_value / len(cuts))
        level = level * jnp.repeat(jnp.exp(steps), shape[axis_at] // blocks).reshape((-1,) + (1,) * (len(shape) - 1 - axis_at))
    return level


def bell_draw(own_key, extent, deviation, limit, pieces=(), held_as=jnp.bfloat16):
    factor_of = steps_of(own_key, extent, pieces, -0.22, 0.18) if pieces else 1.0
    result = jax.random.normal(own_key, extent, jnp.float32) * deviation * factor_of
    return jnp.minimum(jnp.maximum(result, -limit), limit).astype(held_as)


def setup_inputs(seed: int = 0) -> dict:
    splits = jax.random.split(jax.random.key(seed), 11)
    homolog_activations = bell_draw(splits[0], (HOMOLOG_COUNT, CHAIN_LENGTH, FEATURE_DEPTH), 1.0, 6.0, ((0, 4), (1, 64)))
    present_entry_flags = draw_present_entry_flags(jax.random.fold_in(splits[10], 71), 0)
    normalizer_scale = jnp.clip(1.0 + 0.1 * jax.random.normal(splits[2], (FEATURE_DEPTH,), jnp.float32), 0.5, 1.5)
    normalizer_shift = bell_draw(splits[3], (FEATURE_DEPTH,), 0.3, 1.5, (), jnp.float32)
    first_factor_weights = bell_draw(splits[4], (FEATURE_DEPTH, FACTOR_WIDTH), FEATURE_DEPTH ** -0.5, 0.75)
    first_factor_offset = bell_draw(splits[5], (FACTOR_WIDTH,), 0.15, 0.9, (), jnp.float32)
    second_factor_weights = bell_draw(splits[6], (FEATURE_DEPTH, FACTOR_WIDTH), FEATURE_DEPTH ** -0.5, 0.75)
    second_factor_offset = bell_draw(splits[7], (FACTOR_WIDTH,), 0.15, 0.9, (), jnp.float32)
    pairwise_readout_weights = bell_draw(splits[8], (FACTOR_WIDTH * FACTOR_WIDTH, CZ), 0.5, 3.0)
    pairwise_features = bell_draw(splits[9], (CHAIN_LENGTH, CHAIN_LENGTH, CZ), 0.5, 3.0, ((0, 64), (1, 4)))
    return {"homolog_activations": homolog_activations, "present_entry_flags": present_entry_flags, "normalizer_scale": normalizer_scale, "normalizer_shift": normalizer_shift, "first_factor_weights": first_factor_weights, "first_factor_offset": first_factor_offset, "second_factor_weights": second_factor_weights, "second_factor_offset": second_factor_offset, "pairwise_readout_weights": pairwise_readout_weights, "pairwise_features": pairwise_features}


def paired_factors(homolog_activations, present_entry_flags, normalizer_scale, normalizer_shift, first_factor_weights, first_factor_offset, second_factor_weights, second_factor_offset):
    standardized_features = homolog_activations.astype(jnp.float32)
    center = lax.optimization_barrier(jnp.mean(standardized_features, axis=-1, keepdims=True))
    spread = lax.optimization_barrier(jnp.mean((standardized_features - center) ** 2, axis=-1, keepdims=True))
    normed = ((standardized_features - center) * lax.rsqrt(spread + 1e-05) * normalizer_scale + normalizer_shift).astype(jnp.bfloat16)
    flat = normed.reshape(-1, normed.shape[-1])
    masked_input = present_entry_flags.astype(jnp.float32)[..., None]
    first_factor_features = jnp.dot(flat, first_factor_weights, preferred_element_type=jnp.float32).reshape(normed.shape[:-1] + (-1,))
    second_factor_features = jnp.dot(flat, second_factor_weights, preferred_element_type=jnp.float32).reshape(normed.shape[:-1] + (-1,))
    first_factor_features = ((first_factor_features + first_factor_offset) * masked_input).astype(jnp.bfloat16)
    second_factor_features = ((second_factor_features + second_factor_offset) * masked_input).astype(jnp.bfloat16)
    return (first_factor_features, second_factor_features)

def reference(homolog_activations, present_entry_flags, normalizer_scale, normalizer_shift, first_factor_weights, first_factor_offset, second_factor_weights, second_factor_offset, pairwise_readout_weights, pairwise_features):
    first_factor_features, second_factor_features = paired_factors(homolog_activations, present_entry_flags, normalizer_scale, normalizer_shift, first_factor_weights, first_factor_offset, second_factor_weights, second_factor_offset)
    width = first_factor_features.shape[-1]
    weight_wide = pairwise_readout_weights.astype(jnp.float32)
    right_flat = second_factor_features.reshape(HOMOLOG_COUNT, CHAIN_LENGTH * width)
    flat_mask_rows = present_entry_flags.astype(jnp.bfloat16)
    blocks = CHAIN_LENGTH // RES_DEV

    def one_block(index):
        start = (index * RES_DEV).astype(jnp.int32)
        rows = lax.dynamic_slice_in_dim(first_factor_features, start, RES_DEV, 1).reshape(HOMOLOG_COUNT, RES_DEV * width)
        outer = lax.dot_general(rows, right_flat, (((0,), (0,)), ((), ())), preferred_element_type=jnp.float32)
        outer = outer.reshape(RES_DEV, width, CHAIN_LENGTH, width).transpose(0, 2, 1, 3).reshape(RES_DEV * CHAIN_LENGTH, width * width)
        projected = jnp.dot(outer, weight_wide, precision=lax.Precision.HIGHEST).reshape(RES_DEV, CHAIN_LENGTH, -1)
        sequence_row_mask = lax.dynamic_slice_in_dim(flat_mask_rows, start, RES_DEV, 1)
        count = lax.dot_general(sequence_row_mask, flat_mask_rows, (((0,), (0,)), ((), ())), preferred_element_type=jnp.float32)
        return projected / (0.001 + count)[..., None]
    update = lax.map(one_block, jnp.arange(blocks, dtype=jnp.int32)).reshape(CHAIN_LENGTH, CHAIN_LENGTH, -1)
    return (pairwise_features.astype(jnp.float32) + update).astype(jnp.bfloat16)
```

```python
import functools

import jax
import jax.numpy as jnp
from jax import lax
from jax.experimental import pallas as pl
from jax.experimental.pallas import tpu as pltpu
from jax.sharding import PartitionSpec as P

MESH = pl.DeviceIdType.MESH
NT = (((1,), (1,)), ((), ()))

RING_UP, RING_DOWN = 0, 4
FAR, MATE, Y_UP_A, Y_DN_A, Y_UP_B, Y_DN_B, OPP_A, OPP_B = range(8)
CROSS, FLAG_L, FLAG_R = 24, 25, 26
CORE, OUT = 27, 31
N_SEMS = 43


def place(x, y, z, k):
    return ((z // 4) * 2 + k, (x * 4 + y) * 4 + z % 4)


def kernel(
    lin, rin, fin, w2, out, lc, rown, rb, xs, rcs, stage, send_core, got_core, obuf, orecv, ssem, rsem
):
    seq, res = lax.axis_index("seq"), lax.axis_index("res")
    h, k = seq // 2, seq % 2
    x, y, zl = res // 16, (res // 4) % 4, res % 4
    z = h * 4 + zl
    up_z, dn_z = place(x, y, (z + 1) % 8, k), place(x, y, (z + 7) % 8, k)
    anti, sib = place(x, y, (z + 4) % 8, k), place(x, y, z, 1 - k)
    up_y, dn_y = place(x, (y + 1) % 4, z, k), place(x, (y + 3) % 4, z, k)
    odd = x % 2
    mate = place((x + 1 + 2 * odd) % 4, y, z, k)
    far = place((x + 3 + 2 * odd) % 4, y, z, k)
    line = [place(x, y, h * 4 + (zl + d) % 4, k) for d in (1, 2, 3)]
    p = (x - 2 * h + 4) % 4
    source = p < 2
    a = ((p + 1) // 2) % 2
    b = 1 - a

    def copy(src, dst, sem, dev):
        return pltpu.make_async_remote_copy(
            src_ref=src,
            dst_ref=dst,
            send_sem=ssem.at[sem],
            recv_sem=rsem.at[sem],
            device_id=dev,
            device_id_type=MESH,
        )

    def same(ref, sem, dev):
        return copy(ref, ref, sem, dev)

    barrier = pltpu.get_barrier_semaphore()
    partners = [up_z, dn_z, anti, sib, up_y, dn_y, mate, far] + line
    for dev in partners:
        pl.semaphore_signal(barrier, inc=1, device_id=dev, device_id_type=MESH)

    mine = pl.ds(pl.multiple_of(zl * 16, 16), 16)
    lc[h, 0:32, mine, :] = lin[...]
    lc[h, 32, mine, :] = fin[...]
    rown[0:384, :] = rin[...]
    rown[384:400, :] = fin[...]
    pl.semaphore_wait(barrier, len(partners))

    flag_l = copy(fin, lc.at[h, 33, mine, :], FLAG_L, sib)
    flag_r = copy(fin, rown.at[pl.ds(400, 16), :], FLAG_R, sib)
    flag_l.start()
    flag_r.start()
    flag_l.wait()
    flag_r.wait()

    def lslot(zz, lo=0, n=34):
        return lc.at[zz // 4, pl.ds(lo, n), pl.ds(pl.multiple_of((zz % 4) * 16, 16), 16), :]

    def ring(step, zz, up):
        if step == 4:
            part = (0, 17) if up else (17, 17)
        else:
            part = (0, 34)
        sem = (RING_UP if up else RING_DOWN) + step - 1
        return same(lslot(zz, *part), sem, up_z if up else dn_z)

    def rs(n, which, yy):
        return rb.at[n, which, yy % 4]

    def right(n, what, ref, dev):
        return same(ref, 8 + 8 * n + what, dev)

    def far_a(n):
        return right(n, FAR, rs(n, a, y), far)

    def mate_a(n):
        return right(n, MATE, rs(n, a, y), mate)

    def y_copies(n, which):
        ref = rs(n, a if which == 0 else b, y)
        u, d = (Y_UP_A, Y_DN_A) if which == 0 else (Y_UP_B, Y_DN_B)
        return [right(n, u, ref, up_y), right(n, d, ref, dn_y)]

    def opp_a(n):
        return right(n, OPP_A, rs(n, a, y + 3), up_y)

    def opp_b(n):
        return right(n, OPP_B, rs(n, b, y + 1), dn_y)

    def spread_a(n):
        mate_a(n).start()
        for c in y_copies(n, 0):
            c.start()

    def spread_b(n):
        for c in y_copies(n, 1):
            c.start()

    cross = copy(rown, rb.at[1, odd, y], CROSS, anti)

    @pl.when(jnp.logical_not(source))
    def _():
        cross.start()

    @pl.when(source)
    def _():
        rb[0, odd, y] = rown[...]
        far_a(0).start()
        spread_a(0)

    ring(1, z, True).start()
    ring(1, z, False).start()

    @pl.when(jnp.logical_not(source))
    def _():
        right(0, FAR, rs(0, a, y), far).wait_recv()
        spread_a(0)

    right(0, MATE, rs(0, b, y), mate).wait_recv()
    spread_b(0)

    def ring_on(step):
        ring(step, (z + 8 - step) % 8, True).wait_recv()
        ring(step + 1, (z + 8 - step) % 8, True).start()
        ring(step, (z + step) % 8, False).wait_recv()
        ring(step + 1, (z + step) % 8, False).start()

    ring_on(1)

    @pl.when(source)
    def _():
        cross.wait_recv()
        far_a(1).start()
        spread_a(1)

    @pl.when(jnp.logical_not(source))
    def _():
        right(1, FAR, rs(1, a, y), far).wait_recv()
        spread_a(1)

    right(1, MATE, rs(1, b, y), mate).wait_recv()
    spread_b(1)
    ring_on(2)

    for n in range(2):
        right(n, Y_UP_A, rs(n, a, y + 3), up_y).wait_recv()
        opp_a(n).start()
        right(n, Y_DN_B, rs(n, b, y + 1), dn_y).wait_recv()
        opp_b(n).start()
        if n == 0:
            ring_on(3)
    ring(4, (z + 4) % 8, True).wait_recv()
    ring(4, (z + 4) % 8, False).wait_recv()

    low = lax.broadcasted_iota(jnp.int32, (128, 128), 1) < 64

    def block(which, yy, dst):
        def tile(n, carry):
            o = None
            for part in range(2):
                lt = lc[h if part == 0 else 1 - h, pl.ds(n * 4, 4), :, :].reshape(256, 256)
                t = lax.dot_general(
                    rb[part, which, yy, 0:384, :], lt, NT, preferred_element_type=jnp.float32
                )
                o = t if o is None else o + t
            ob = o.astype(jnp.bfloat16).reshape(6, 2, 32, 256)
            for jj in range(2):
                for cl in range(2):
                    rows = pl.ds(pl.multiple_of(n * 64 + cl * 32, 32), 32)
                    xs[:, rows, jj * 128 : jj * 128 + 128] = ob[:, jj, :, cl * 128 : cl * 128 + 128]
            return carry

        lax.fori_loop(0, 8, tile, 0)
        cnt = jnp.zeros((16, 128), jnp.float32)
        for part in range(2):
            for core in range(2):
                lf = lc[h if part == 0 else 1 - h, 32 + core, :, :]
                cnt += lax.dot_general(
                    rb[part, which, yy, 384 + 16 * core : 400 + 16 * core, :],
                    jnp.concatenate([lf, lf], axis=0),
                    NT,
                    preferred_element_type=jnp.float32,
                )
        rcs[...] = 1.0 / (0.001 + cnt)

        def pair(jp, carry):
            q = jnp.dot(w2[...], xs[jp], preferred_element_type=jnp.float32)
            for jj in range(2):
                j = 2 * jp + jj
                c = jnp.where(low, q[:128, jj * 128 : jj * 128 + 128], q[128:, jj * 128 : jj * 128 + 128])
                t = (c * rcs[pl.ds(j, 1), :]).T
                s = t[:64] + t[64:]
                for zi in range(4):
                    dst[pl.ds(zi * 144 + j, 12, stride=12), :] = s[zi * 16 : zi * 16 + 12]
            return carry

        lax.fori_loop(0, 6, pair, 0)

    steps = (0, 3, 1, 2)
    for s, off in enumerate(steps):
        yy = (y + off) % 4
        if off == 3:
            for n in range(2):
                right(n, Y_UP_B, rs(n, b, yy), up_y).wait_recv()
        if off == 1:
            for n in range(2):
                right(n, Y_DN_A, rs(n, a, yy), dn_y).wait_recv()
        if off == 2:
            for n in range(2):
                right(n, OPP_A, rs(n, a, yy), up_y).wait_recv()
                right(n, OPP_B, rs(n, b, yy), dn_y).wait_recv()
        swap = copy(send_core.at[s], got_core.at[s], CORE + s, sib)
        block(1 - k, yy, send_core.at[s])
        swap.start()
        block(k, yy, stage)
        swap.wait_recv()
        obuf[s] = (stage[...] + got_core[s]).astype(jnp.bfloat16).reshape(4, 144, 128)
        for d in range(3):
            zi = (zl + d + 1) % 4
            copy(obuf.at[s, zi], orecv.at[zl, yy], OUT + 3 * s + d, line[d]).start()
        orecv[zl, yy] = obuf[s, zl]

    for s, off in enumerate(steps):
        yy = (y + off) % 4
        for d in range(3):
            zi = (zl + d + 1) % 4
            src = (zl + 3 - d) % 4
            copy(obuf.at[s, zi], orecv.at[src, yy], OUT + 3 * s + d, line[d]).wait()
        copy(send_core.at[s], got_core.at[s], CORE + s, sib).wait_send()
    out[...] = orecv[...]

    for step in range(1, 5):
        ring(step, (z + 9 - step) % 8, True).wait_send()
        ring(step, (z + step - 1) % 8, False).wait_send()
    for n in range(2):
        for c in [mate_a(n)] + y_copies(n, 0) + y_copies(n, 1) + [opp_a(n), opp_b(n)]:
            c.wait_send()

    @pl.when(source)
    def _():
        far_a(0).wait_send()
        far_a(1).wait_send()

    @pl.when(jnp.logical_not(source))
    def _():
        cross.wait_send()


def exchange(lin, rin, fin, w2):
    bf, f32 = jnp.bfloat16, jnp.float32
    vm = pl.BlockSpec(memory_space=pltpu.VMEM)
    return pl.pallas_call(
        kernel,
        out_shape=jax.ShapeDtypeStruct((4, 4, 144, 128), bf),
        in_specs=[vm] * 4,
        out_specs=vm,
        scratch_shapes=[
            pltpu.VMEM((2, 34, 64, 256), bf),
            pltpu.VMEM((416, 256), bf),
            pltpu.VMEM((2, 2, 4, 416, 256), bf),
            pltpu.VMEM((6, 512, 256), bf),
            pltpu.VMEM((16, 128), f32),
            pltpu.VMEM((576, 128), f32),
            pltpu.VMEM((4, 576, 128), f32),
            pltpu.VMEM((4, 576, 128), f32),
            pltpu.VMEM((4, 4, 144, 128), bf),
            pltpu.VMEM((4, 4, 144, 128), bf),
            pltpu.SemaphoreType.DMA((N_SEMS,)),
            pltpu.SemaphoreType.DMA((N_SEMS,)),
        ],
        compiler_params=pltpu.CompilerParams(
            collective_id=0, has_side_effects=True, vmem_limit_bytes=48 * 2**20
        ),
        name="outer_mean",
    )(lin, rin, fin, w2)


def body(msa, flags, scale, shift, w_left, b_left, w_right, b_right, readout, pair):
    f32, bf = jnp.float32, jnp.bfloat16
    v = msa.astype(f32)
    center = jnp.mean(v, axis=-1, keepdims=True)
    spread = jnp.mean((v - center) ** 2, axis=-1, keepdims=True)
    normed = ((v - center) * lax.rsqrt(spread + 1e-05) * scale + shift).astype(bf)
    mask = flags.astype(f32).T
    left = jnp.einsum("sid,dc->cis", normed, w_left, preferred_element_type=f32)
    left = ((left + b_left[:, None, None]) * mask[None]).astype(bf)
    right = jnp.einsum("sid,de->ies", normed, w_right, preferred_element_type=f32)
    right = ((right + b_right[None, :, None]) * mask[:, None, :]).astype(bf)
    lin = jnp.pad(left, ((0, 0), (0, 4), (0, 0)))
    rin = right.reshape(384, 256)
    fin = jnp.pad(mask.astype(bf), ((0, 4), (0, 0)))
    w2 = readout.reshape(16, 2, 32, 128).transpose(1, 3, 0, 2).reshape(256, 512)
    got = exchange(lin, rin, fin, w2)
    update = got.reshape(4, 4, 12, 12, 128).transpose(2, 1, 0, 3, 4).reshape(12, 192, 128)
    return (pair.astype(f32) + update.astype(f32)).astype(bf)


def solution(mesh):
    in_specs = (
        P("seq", "res", None),
        P("seq", "res"),
        P(),
        P(),
        P(),
        P(),
        P(),
        P(),
        P(),
        P("res", "seq", None),
    )
    return jax.shard_map(
        body, mesh=mesh, in_specs=in_specs, out_specs=P("res", "seq", None), check_vma=False
    )
```

```python
import functools

import jax
import jax.numpy as jnp
from jax import lax
from jax.experimental import pallas as pl
from jax.experimental.pallas import tpu as pltpu
from jax.sharding import PartitionSpec as P

MESH = pl.DeviceIdType.MESH
NT = (((1,), (1,)), ((), ()))
BF, F32 = jnp.bfloat16, jnp.float32

RING_UP, RING_DOWN = 0, 4
FAR, MATE, Y_UP_A, Y_DN_A, Y_UP_B, Y_DN_B, OPP, MATE_OPP = range(8)
CROSS, CORE, COUNT, OUT = 24, 25, 29, 33
N_SEMS = 45
STEPS = (0, 3, 1, 2)
BLOCK = 400


def place(x, y, z, k):
    return ((z // 4) * 2 + k, (x * 4 + y) * 4 + z % 4)


def kernel(
    msa, flags, vecs, w12, readout, out,
    lown, rown, lp, lc, lf, wide, rb, w2, xs, cnt, got_cnt, rcs, stage, send_core, got_core, obuf, orecv,
    ssem, rsem,
):
    seq, res = lax.axis_index("seq"), lax.axis_index("res")
    h, k = seq // 2, seq % 2
    x, y, zl = res // 16, (res // 4) % 4, res % 4
    z = h * 4 + zl
    up_z, dn_z = place(x, y, (z + 1) % 8, k), place(x, y, (z + 7) % 8, k)
    anti, sib = place(x, y, (z + 4) % 8, k), place(x, y, z, 1 - k)
    up_y, dn_y = place(x, (y + 1) % 4, z, k), place(x, (y + 3) % 4, z, k)
    odd = x % 2
    mate = place((x + 1 + 2 * odd) % 4, y, z, k)
    far = place((x + 3 + 2 * odd) % 4, y, z, k)
    line = [place(x, y, h * 4 + (zl + d) % 4, k) for d in (1, 2, 3)]
    p = (x - 2 * h + 4) % 4
    source = p < 2
    a = ((p + 1) // 2) % 2
    b = 1 - a

    def copy(src, dst, sem, dev):
        return pltpu.make_async_remote_copy(
            src_ref=src,
            dst_ref=dst,
            send_sem=ssem.at[sem],
            recv_sem=rsem.at[sem],
            device_id=dev,
            device_id_type=MESH,
        )

    def same(ref, sem, dev):
        return copy(ref, ref, sem, dev)

    barrier = pltpu.get_barrier_semaphore()
    partners = [up_z, dn_z, anti, sib, up_y, dn_y, mate, far] + line
    for dev in partners:
        pl.semaphore_signal(barrier, inc=1, device_id=dev, device_id_type=MESH)

    scale, shift, offset = vecs[:, 0:1], vecs[:, 1:2], vecs[:, 2:3]

    def residue(i, carry):
        v = msa[i].astype(F32)
        c = v - jnp.mean(v, axis=0, keepdims=True)
        var = jnp.mean(c * c, axis=0, keepdims=True)
        normed = (c * lax.rsqrt(var + 1e-05) * scale + shift).astype(BF)
        both = jnp.dot(w12[...], normed, preferred_element_type=F32)
        both = ((both + offset) * flags[pl.ds(i, 1), :].astype(F32)).astype(BF)
        rows = pl.ds(pl.multiple_of(i * 32, 32), 32)
        lown[rows, :] = both[:32]
        rown[rows, :] = both[32:]
        return carry

    lax.fori_loop(0, 12, residue, 0, unroll=6)
    mask = jnp.concatenate([flags[...].astype(F32), jnp.zeros((4, 256), F32)], axis=0).astype(BF)
    lown[384:400, :] = mask
    rown[384:400, :] = mask
    wide[:, 384:512, :] = jnp.zeros((2, 128, 128), F32)
    pl.semaphore_wait(barrier, len(partners))

    def ring(step, zz, up):
        lo, n = (0, BLOCK) if step < 4 else (0, 208) if up else (208, 192)
        sem = (RING_UP if up else RING_DOWN) + step - 1
        dst = lp.at[zz, pl.ds(lo, n), :]
        src = lown.at[pl.ds(lo, n), :] if step == 1 else dst
        return copy(src, dst, sem, up_z if up else dn_z)

    def repack(src, zz):
        part, at = (zz // 4 + h) % 2, pl.ds(pl.multiple_of((zz % 4) * 16, 16), 16)
        for half in range(2):
            lanes = slice(half * 128, half * 128 + 128)
            wide[half, 0:384, :] = src[0:384, lanes].astype(F32)
            for c in range(32):
                lc[part, c, at, lanes] = wide[half, pl.ds(c, 16, stride=32), :].astype(BF)
        lf[part, at, :] = src[384:400, :]

    def ring_on(step, up):
        zz = (z + 8 - step) % 8 if up else (z + step) % 8
        ring(step, zz, up).wait_recv()
        ring(step + 1, zz, up).start()

    def ring_repack(step):
        repack(lp.at[(z + 8 - step) % 8], (z + 8 - step) % 8)
        repack(lp.at[(z + step) % 8], (z + step) % 8)

    def rs(n, which, yy):
        return rb.at[n, which, yy % 4]

    def right(n, what, which, yy, dev):
        return same(rs(n, which, yy), 8 + 8 * n + what, dev)

    def far_a(n):
        return right(n, FAR, a, y, far)

    def mate_a(n):
        return right(n, MATE, a, y, mate)

    def y_copies(n, which):
        u, d = (Y_UP_A, Y_DN_A) if which == 0 else (Y_UP_B, Y_DN_B)
        side = a if which == 0 else b
        return [right(n, u, side, y, up_y), right(n, d, side, y, dn_y)]

    def opp_y(n):
        return right(n, OPP, a, y + 3, up_y) if n == 0 else right(n, OPP, a, y + 1, dn_y)

    def opp_far(n):
        return right(n, OPP, a, y + 2, far)

    def opp_mate(n):
        return right(n, MATE_OPP, a, y + 2, mate)

    def wait(n, what):
        which, yy = {
            FAR: (a, y), MATE: (b, y), Y_UP_A: (a, y + 3), Y_DN_A: (a, y + 1), Y_UP_B: (b, y + 3),
            Y_DN_B: (b, y + 1), OPP: (a, y + 2), MATE_OPP: (b, y + 2),
        }[what]
        right(n, what, which, yy, sib).wait_recv()

    def spread_b(n):
        wait(n, MATE)
        for c in y_copies(n, 1):
            c.start()

    cross = copy(rown, rb.at[1, odd, y], CROSS, anti)

    @pl.when(source)
    def _():
        rb[0, odd, y] = rown[...]
        far_a(0).start()
        mate_a(0).start()
        for c in y_copies(0, 0):
            c.start()
        ring(1, z, True).start()
        ring(1, z, False).start()
        spread_b(0)
        wait(0, Y_UP_A)
        opp_y(0).start()
        ring_on(1, True)
        ring_on(1, False)
        cross.wait_recv()
        far_a(1).start()
        mate_a(1).start()
        for c in y_copies(1, 0):
            c.start()
        wait(0, OPP)
        opp_far(0).start()
        opp_mate(0).start()

    @pl.when(jnp.logical_not(source))
    def _():
        cross.start()
        ring(1, z, True).start()
        ring(1, z, False).start()
        wait(0, FAR)
        mate_a(0).start()
        for c in y_copies(0, 0):
            c.start()
        ring_on(1, True)
        ring_on(1, False)
        spread_b(0)

    repack(lown, z)
    ring_repack(1)
    for cp in range(16):
        w2[:, cp * 32 : cp * 32 + 32] = jnp.concatenate(
            [readout[cp * 64 : cp * 64 + 32, :].T, readout[cp * 64 + 32 : cp * 64 + 64, :].T], axis=0
        )
    ring_on(2, True)
    ring_on(2, False)

    @pl.when(source)
    def _():
        spread_b(1)
        wait(1, Y_DN_A)
        opp_y(1).start()

    @pl.when(jnp.logical_not(source))
    def _():
        wait(1, FAR)
        mate_a(1).start()
        for c in y_copies(1, 0):
            c.start()
        wait(0, OPP)
        opp_mate(0).start()

    ring_repack(2)
    ring_on(3, True)
    ring_on(3, False)

    @pl.when(jnp.logical_not(source))
    def _():
        spread_b(1)

    @pl.when(source)
    def _():
        wait(1, OPP)
        opp_far(1).start()
        opp_mate(1).start()

    ring_repack(3)
    ring(4, (z + 4) % 8, True).wait_recv()
    ring(4, (z + 4) % 8, False).wait_recv()
    repack(lp.at[(z + 4) % 8], (z + 4) % 8)

    low = lax.broadcasted_iota(jnp.int32, (128, 128), 1) < 64

    def counts(s, yy):
        for which in range(2):
            t = jnp.zeros((16, 128), F32)
            for part in range(2):
                two = jnp.concatenate([lf[part], lf[part]], axis=0)
                t += lax.dot_general(
                    rb[part, which, yy, 384:400, :], two, NT, preferred_element_type=F32
                )
            cnt[s, which] = t

    def multiply(which, yy):
        def tile(n, carry):
            o = None
            for part in range(2):
                lt = lc[part, pl.ds(n * 4, 4), :, :].reshape(256, 256)
                t = lax.dot_general(rb[part, which, yy, 0:384, :], lt, NT, preferred_element_type=F32)
                o = t if o is None else o + t
            ob = o.astype(BF).reshape(6, 2, 32, 256)
            for jj in range(2):
                for cl in range(2):
                    rows = pl.ds(pl.multiple_of(n * 64 + cl * 32, 32), 32)
                    xs[:, rows, jj * 128 : jj * 128 + 128] = ob[:, jj, :, cl * 128 : cl * 128 + 128]
            return carry

        lax.fori_loop(0, 8, tile, 0, unroll=True)

    def project(dst):
        def pair(jp, carry):
            q = jnp.dot(w2[...], xs[jp], preferred_element_type=F32)
            for jj in range(2):
                j = 2 * jp + jj
                c = jnp.where(low, q[:128, jj * 128 : jj * 128 + 128], q[128:, jj * 128 : jj * 128 + 128])
                t = (c * rcs[pl.ds(j, 1), :]).T
                s = t[:64] + t[64:]
                for zi in range(4):
                    dst[pl.ds(zi * 144 + j, 12, stride=12), :] = s[zi * 16 : zi * 16 + 12]
            return carry

        lax.fori_loop(0, 6, pair, 0, unroll=True)

    for s, off in enumerate(STEPS):
        yy = (y + off) % 4
        if off == 3:
            for n in range(2):
                if n == 0:

                    @pl.when(jnp.logical_not(source))
                    def _():
                        wait(0, Y_UP_A)
                else:
                    wait(1, Y_UP_A)
                wait(n, Y_UP_B)
        if off == 1:
            for n in range(2):
                if n == 1:

                    @pl.when(jnp.logical_not(source))
                    def _():
                        wait(1, Y_DN_A)
                else:
                    wait(0, Y_DN_A)
                wait(n, Y_DN_B)
        if off == 2:
            for n in range(2):
                wait(n, MATE_OPP)
        swap = copy(send_core.at[s], got_core.at[s], CORE + s, sib)
        counts(s, yy)
        swap_counts = copy(cnt.at[s], got_cnt.at[s], COUNT + s, sib)
        swap_counts.start()
        multiply(1 - k, yy)
        swap_counts.wait()
        rcs[...] = 1.0 / (0.001 + cnt[s, 1 - k] + got_cnt[s, 1 - k])
        project(send_core.at[s])
        swap.start()
        if off == 0:

            @pl.when(jnp.logical_not(source))
            def _():
                wait(1, OPP)
                opp_mate(1).start()

        rcs[...] = 1.0 / (0.001 + cnt[s, k] + got_cnt[s, k])
        multiply(k, yy)
        project(stage)
        swap.wait_recv()
        obuf[s] = (stage[...] + got_core[s]).astype(BF).reshape(4, 144, 128)
        for d in range(3):
            zi = (zl + d + 1) % 4
            copy(obuf.at[s, zi], orecv.at[zl, yy], OUT + 3 * s + d, line[d]).start()
        orecv[zl, yy] = obuf[s, zl]

    for s, off in enumerate(STEPS):
        yy = (y + off) % 4
        for d in range(3):
            zi = (zl + d + 1) % 4
            src = (zl + 3 - d) % 4
            copy(obuf.at[s, zi], orecv.at[src, yy], OUT + 3 * s + d, line[d]).wait()
        copy(send_core.at[s], got_core.at[s], CORE + s, sib).wait_send()
    out[...] = orecv[...]

    for step in range(1, 5):
        ring(step, (z + 9 - step) % 8, True).wait_send()
        ring(step, (z + step - 1) % 8, False).wait_send()
    for n in range(2):
        for c in [mate_a(n), opp_mate(n)] + y_copies(n, 0) + y_copies(n, 1):
            c.wait_send()

    @pl.when(source)
    def _():
        for n in range(2):
            for c in [far_a(n), opp_y(n), opp_far(n)]:
                c.wait_send()

    @pl.when(jnp.logical_not(source))
    def _():
        cross.wait_send()


def exchange(*args):
    vm = pl.BlockSpec(memory_space=pltpu.VMEM)
    return pl.pallas_call(
        kernel,
        out_shape=jax.ShapeDtypeStruct((4, 4, 144, 128), BF),
        in_specs=[vm] * len(args),
        out_specs=vm,
        scratch_shapes=[
            pltpu.VMEM((BLOCK, 256), BF),
            pltpu.VMEM((BLOCK, 256), BF),
            pltpu.VMEM((8, BLOCK, 256), BF),
            pltpu.VMEM((2, 32, 64, 256), BF),
            pltpu.VMEM((2, 64, 256), BF),
            pltpu.VMEM((2, 512, 128), F32),
            pltpu.VMEM((2, 2, 4, BLOCK, 256), BF),
            pltpu.VMEM((256, 512), BF),
            pltpu.VMEM((6, 512, 256), BF),
            pltpu.VMEM((4, 2, 16, 128), F32),
            pltpu.VMEM((4, 2, 16, 128), F32),
            pltpu.VMEM((16, 128), F32),
            pltpu.VMEM((576, 128), F32),
            pltpu.VMEM((4, 576, 128), F32),
            pltpu.VMEM((4, 576, 128), F32),
            pltpu.VMEM((4, 4, 144, 128), BF),
            pltpu.VMEM((4, 4, 144, 128), BF),
            pltpu.SemaphoreType.DMA((N_SEMS,)),
            pltpu.SemaphoreType.DMA((N_SEMS,)),
        ],
        compiler_params=pltpu.CompilerParams(
            collective_id=0, has_side_effects=True, vmem_limit_bytes=48 * 2**20
        ),
        name="outer_mean",
    )(*args)


def body(msa, flags, scale, shift, w_left, b_left, w_right, b_right, readout, pair):
    vecs = jnp.stack([scale, shift, jnp.concatenate([b_left, b_right])], axis=1)
    w12 = jnp.concatenate([w_left.T, w_right.T], axis=0)
    got = exchange(msa.transpose(1, 2, 0), flags.T, vecs, w12, readout)
    update = got.reshape(4, 4, 12, 12, 128).transpose(2, 1, 0, 3, 4).reshape(12, 192, 128)
    return (pair.astype(F32) + update.astype(F32)).astype(BF)


def solution(mesh):
    in_specs = (
        P("seq", "res", None),
        P("seq", "res"),
        P(),
        P(),
        P(),
        P(),
        P(),
        P(),
        P(),
        P("res", "seq", None),
    )
    return jax.shard_map(
        body, mesh=mesh, in_specs=in_specs, out_specs=P("res", "seq", None), check_vma=False
    )
```

```python
import functools

import jax
import jax.numpy as jnp
from jax import lax
from jax.experimental import pallas as pl
from jax.experimental.pallas import tpu as pltpu
from jax.sharding import PartitionSpec as P

MESH = pl.DeviceIdType.MESH
NT = (((1,), (1,)), ((), ()))
BF, F32 = jnp.bfloat16, jnp.float32

RING_UP, RING_DOWN, PLANE = 0, 7, 14
FAR, MATE, Y_UP_A, Y_DN_A, Y_UP_B, Y_DN_B, OPP, MATE_OPP = range(8)
CROSS, CORE, COUNT, OUT = 46, 48, 52, 56
RELAY = 68
N_SEMS = 69
STEPS = (0, 3, 1, 2)
BLOCK = 400
HALVES = ((0, 208), (208, 192))


def place(x, y, z, k):
    return ((z // 4) * 2 + k, (x * 4 + y) * 4 + z % 4)


def kernel(
    msa_in, flags_in, scale_in, shift_in, w_left_in, b_left_in, w_right_in, b_right_in, readout_in, pair, out,
    lown, rown, lp, lc, lf, wide, rb, w2, xs, cnt, got_cnt, rcs, stage, send_core, got_core, obuf, orecv,
    w12, pairs, relay, msa, flags, scale, shift, w_left, b_left, w_right, b_right, readout, ssem, rsem, lsem,
):
    seq, res = lax.axis_index("seq"), lax.axis_index("res")
    h, k = seq // 2, seq % 2
    x, y, zl = res // 16, (res // 4) % 4, res % 4
    z = h * 4 + zl
    up_z, dn_z = place(x, y, (z + 1) % 8, k), place(x, y, (z + 7) % 8, k)
    anti, sib = place(x, y, (z + 4) % 8, k), place(x, y, z, 1 - k)
    up_y, dn_y = place(x, (y + 1) % 4, z, k), place(x, (y + 3) % 4, z, k)
    odd = x % 2
    mate = place((x + 1 + 2 * odd) % 4, y, z, k)
    far = place((x + 3 + 2 * odd) % 4, y, z, k)
    line = [place(x, y, h * 4 + (zl + d) % 4, k) for d in (1, 2, 3)]
    p = (x - 2 * h + 4) % 4
    source = p < 2
    a = ((p + 1) // 2) % 2
    b = 1 - a

    def copy(src, dst, sem, dev):
        return pltpu.make_async_remote_copy(
            src_ref=src,
            dst_ref=dst,
            send_sem=ssem.at[sem],
            recv_sem=rsem.at[sem],
            device_id=dev,
            device_id_type=MESH,
        )

    def same(ref, sem, dev):
        return copy(ref, ref, sem, dev)

    barrier = pltpu.get_barrier_semaphore()
    partners = [up_z, dn_z, anti, sib, up_y, dn_y, mate, far] + line
    for dev in partners:
        pl.semaphore_signal(barrier, inc=1, device_id=dev, device_id_type=MESH)

    loads = [
        pltpu.make_async_copy(src, dst, lsem.at[i])
        for i, (src, dst) in enumerate((
            (msa_in, msa), (flags_in, flags), (scale_in, scale), (shift_in, shift), (w_left_in, w_left),
            (b_left_in, b_left), (w_right_in, w_right), (b_right_in, b_right), (readout_in, readout), (pair, pairs),
        ))
    ]
    for load in loads:
        load.start()
    for load in loads[:8]:
        load.wait()
    w12[0:32, :] = w_left[...]
    w12[32:64, :] = w_right[...]

    def column(row):
        square = (row.shape[1], row.shape[1])
        diagonal = lax.broadcasted_iota(jnp.int32, square, 0) == lax.broadcasted_iota(jnp.int32, square, 1)
        return jnp.sum(jnp.where(diagonal, row, 0.0), axis=1, keepdims=True)

    gain, bias = column(scale[...]), column(shift[...])
    offset = jnp.concatenate([column(b_left[...]), column(b_right[...])], axis=0)

    def residue(i, carry):
        v = msa[i].astype(F32)
        c = v - jnp.mean(v, axis=0, keepdims=True)
        var = jnp.mean(c * c, axis=0, keepdims=True)
        normed = (c * lax.rsqrt(var + 1e-05) * gain + bias).astype(BF)
        both = jnp.dot(w12[...], normed, preferred_element_type=F32)
        both = ((both + offset) * flags[pl.ds(i, 1), :].astype(F32)).astype(BF)
        rows = pl.ds(pl.multiple_of(i * 32, 32), 32)
        lown[rows, :] = both[:32]
        rown[rows, :] = both[32:]
        return carry

    lax.fori_loop(0, 12, residue, 0, unroll=6)
    mask = jnp.concatenate([flags[...].astype(F32), jnp.zeros((4, 256), F32)], axis=0).astype(BF)
    lown[384:400, :] = mask
    rown[384:400, :] = mask
    wide[:, 384:512, :] = jnp.zeros((2, 128, 128), F32)
    pl.semaphore_wait(barrier, len(partners))

    def ring(step, zz, up, c):
        sem = (RING_UP if up else RING_DOWN) + 2 * (step - 1) + (c if step < 4 else 0)
        dst = lp.at[zz, pl.ds(*HALVES[c]), :]
        src = lown.at[pl.ds(*HALVES[c]), :] if step == 1 else dst
        return copy(src, dst, sem, up_z if up else dn_z)

    def ring_pieces(step):
        return [(up, c) for c in range(2) for up in (True, False) if step < 4 or up == (c == 0)]

    def ring_from(step, up):
        return (z + 8 - step) % 8 if up else (z + step) % 8

    def ring_on(step, c):
        for up in (True, False):
            ring(step, ring_from(step, up), up, c).wait_recv()
            if (up, c) in ring_pieces(step + 1):
                ring(step + 1, ring_from(step, up), up, c).start()

    def repack(src, zz):
        part, at = (zz // 4 + h) % 2, pl.ds(pl.multiple_of((zz % 4) * 16, 16), 16)
        for half in range(2):
            lanes = slice(half * 128, half * 128 + 128)
            wide[half, 0:384, :] = src[0:384, lanes].astype(F32)
            for c in range(32):
                lc[part, c, at, lanes] = wide[half, pl.ds(c, 16, stride=32), :].astype(BF)
        lf[part, at, :] = src[384:400, :]

    def ring_repack(step):
        repack(lp.at[(z + 8 - step) % 8], (z + 8 - step) % 8)
        repack(lp.at[(z + step) % 8], (z + step) % 8)

    def right(n, what, which, yy, dev, c):
        ref = rb.at[n, which, yy % 4, pl.ds(*HALVES[c]), :]
        return same(ref, PLANE + 2 * (8 * n + what) + c, dev)

    def far_a(n, c):
        return right(n, FAR, a, y, far, c)

    def mate_a(n, c):
        return right(n, MATE, a, y, mate, c)

    def y_copies(n, which, c):
        u, d = (Y_UP_A, Y_DN_A) if which == 0 else (Y_UP_B, Y_DN_B)
        side = a if which == 0 else b
        return [right(n, u, side, y, up_y, c), right(n, d, side, y, dn_y, c)]

    def opp_y(n, c):
        if n == 0:
            return right(n, OPP, a, y + 3, up_y, c)
        return right(n, OPP, a, y + 1, dn_y, c)

    def opp_far(n, c):
        return right(n, OPP, a, y + 2, far, c)

    def opp_mate(n, c):
        return right(n, MATE_OPP, a, y + 2, mate, c)

    def wait(n, what, c):
        which, yy = {
            FAR: (a, y), MATE: (b, y), Y_UP_A: (a, y + 3), Y_DN_A: (a, y + 1), Y_UP_B: (b, y + 3),
            Y_DN_B: (b, y + 1), OPP: (a, y + 2), MATE_OPP: (b, y + 2),
        }[what]
        right(n, what, which, yy, sib, c).wait_recv()

    def start(copies):
        for cp in copies:
            cp.start()

    def on_far(n, c):
        wait(n, FAR, c)
        start([mate_a(n, c)] + y_copies(n, 0, c))

    def on_mate(n, c):
        wait(n, MATE, c)
        start(y_copies(n, 1, c))

    def on_side(n, c):
        wait(n, Y_UP_A if n == 0 else Y_DN_A, c)
        opp_y(n, c).start()

    def on_opp(n, c):
        wait(n, OPP, c)
        start([opp_far(n, c), opp_mate(n, c)])

    def on_opp_far(n, c):
        wait(n, OPP, c)
        opp_mate(n, c).start()

    def cross(c):
        if c == 0:
            return copy(rown.at[pl.ds(*HALVES[0]), :], rb.at[1, odd, y, pl.ds(*HALVES[0]), :], CROSS, anti)
        return copy(relay, rb.at[1, 1 - odd, y, pl.ds(*HALVES[1]), :], CROSS + 1, anti)

    to_relay = copy(rown.at[pl.ds(*HALVES[1]), :], relay, RELAY, far)

    def on_cross(c):
        cross(c).wait_recv()
        start([far_a(1, c), mate_a(1, c)] + y_copies(1, 0, c))

    def prepare():
        loads[8].wait()
        for cp in range(16):
            w2[:, cp * 32 : cp * 32 + 32] = jnp.concatenate(
                [readout[cp * 64 : cp * 64 + 32, :].T, readout[cp * 64 + 32 : cp * 64 + 64, :].T], axis=0
            )
        repack(lown, z)

    @pl.when(source)
    def _():
        rb[0, odd, y] = rown[...]
        for c in range(2):
            start([far_a(0, c), mate_a(0, c)] + y_copies(0, 0, c))
            start([ring(1, z, up, c) for up in (True, False)])
        prepare()
        to_relay.wait_recv()
        cross(1).start()
        for c in range(2):
            on_mate(0, c)
            on_side(0, c)
            ring_on(1, c)
        on_cross(0)
        on_opp(0, 0)
        ring_on(2, 0)
        ring_repack(1)
        on_far(1, 1)
        ring_on(2, 1)
        on_opp(0, 1)
        on_mate(1, 0)
        on_side(1, 0)
        ring_on(3, 0)
        on_mate(1, 1)
        on_side(1, 1)
        ring_repack(2)
        ring_on(3, 1)
        ring_repack(3)

    @pl.when(jnp.logical_not(source))
    def _():
        to_relay.start()
        start([ring(1, z, up, 0) for up in (True, False)])
        cross(0).start()
        start([ring(1, z, up, 1) for up in (True, False)])
        prepare()
        for c in range(2):
            on_far(0, c)
            ring_on(1, c)
        on_mate(0, 0)
        on_cross(1)
        on_mate(0, 1)
        ring_on(2, 0)
        on_far(1, 0)
        ring_repack(1)
        ring_on(2, 1)
        on_opp_far(0, 0)
        on_opp_far(0, 1)
        on_mate(1, 0)
        ring_on(3, 0)
        ring_repack(2)
        on_mate(1, 1)
        ring_on(3, 1)
        ring_repack(3)

    for up, c in ring_pieces(4):
        ring(4, (z + 4) % 8, up, c).wait_recv()
    repack(lp.at[(z + 4) % 8], (z + 4) % 8)

    low = lax.broadcasted_iota(jnp.int32, (128, 128), 1) < 64

    def counts(s, yy):
        for which in range(2):
            t = jnp.zeros((16, 128), F32)
            for part in range(2):
                two = jnp.concatenate([lf[part], lf[part]], axis=0)
                t += lax.dot_general(
                    rb[part, which, yy, 384:400, :], two, NT, preferred_element_type=F32
                )
            cnt[s, which] = t

    def multiply(which, yy, slot):
        def tile(n, carry):
            o = None
            for part in range(2):
                lt = lc[part, pl.ds(n * 4, 4), :, :].reshape(256, 256)
                t = lax.dot_general(rb[part, which, yy, 0:384, :], lt, NT, preferred_element_type=F32)
                o = t if o is None else o + t
            ob = o.astype(BF).reshape(6, 2, 32, 256)
            for jj in range(2):
                for cl in range(2):
                    rows = pl.ds(pl.multiple_of(n * 64 + cl * 32, 32), 32)
                    xs[slot, :, rows, jj * 128 : jj * 128 + 128] = ob[:, jj, :, cl * 128 : cl * 128 + 128]
            return carry

        lax.fori_loop(0, 8, tile, 0, unroll=True)

    def project(dst, slot):
        def pair(jp, carry):
            q = jnp.dot(w2[...], xs[slot, jp], preferred_element_type=F32)
            for jj in range(2):
                j = 2 * jp + jj
                c = jnp.where(low, q[:128, jj * 128 : jj * 128 + 128], q[128:, jj * 128 : jj * 128 + 128])
                t = (c * rcs[pl.ds(j, 1), :]).T
                s = t[:64] + t[64:]
                for zi in range(4):
                    dst[pl.ds(zi * 144 + j, 12, stride=12), :] = s[zi * 16 : zi * 16 + 12]
            return carry

        lax.fori_loop(0, 6, pair, 0, unroll=True)

    def arrive(off):
        for c in range(2):
            for n in range(2):
                if off == 2:
                    wait(n, MATE_OPP, c)
                if off in (1, 3):
                    first, second = (Y_UP_A, Y_UP_B) if off == 3 else (Y_DN_A, Y_DN_B)
                    if n == (0 if off == 3 else 1):

                        @pl.when(jnp.logical_not(source))
                        def _():
                            wait(n, first, c)
                    else:
                        wait(n, first, c)
                    wait(n, second, c)

    def late(c, follow):
        @pl.when(jnp.logical_not(source) if follow else source)
        def _():
            on_opp_far(1, c) if follow else on_opp(1, c)

    def finish(s, off):
        yy = (y + off) % 4
        for d in range(3):
            zi = (zl + d + 1) % 4
            src = (zl + 3 - d) % 4
            copy(obuf.at[s, zi], orecv.at[src, yy], OUT + 3 * s + d, line[d]).wait_recv()
        got = [orecv[q, yy].astype(F32) for q in range(4)]
        at = pl.ds(pl.multiple_of(yy * 48, 16), 48)
        for i in range(12):
            new = jnp.concatenate([g[i * 12 : i * 12 + 12] for g in got], axis=0)
            out[i, at, :] = (pairs[i, at, :].astype(F32) + new).astype(BF)

    for s, off in enumerate(STEPS):
        yy = (y + off) % 4
        arrive(off)
        swap = copy(send_core.at[s], got_core.at[s], CORE + s, sib)
        counts(s, yy)
        swap_counts = copy(cnt.at[s], got_cnt.at[s], COUNT + s, sib)
        swap_counts.start()
        multiply(1 - k, yy, 0)
        if off == 0:
            late(0, False)
            multiply(k, yy, 1)
            late(1, False)
        swap_counts.wait()
        rcs[...] = 1.0 / (0.001 + cnt[s, 1 - k] + got_cnt[s, 1 - k])
        project(send_core.at[s], 0)
        swap.start()
        rcs[...] = 1.0 / (0.001 + cnt[s, k] + got_cnt[s, k])
        if off == 0:
            late(0, True)
        else:
            multiply(k, yy, 1)
            if s == 1:
                late(1, True)
        project(stage, 1)
        swap.wait_recv()
        obuf[s] = (stage[...] + got_core[s]).astype(BF).reshape(4, 144, 128)
        for d in range(3):
            zi = (zl + d + 1) % 4
            copy(obuf.at[s, zi], orecv.at[zl, yy], OUT + 3 * s + d, line[d]).start()
        orecv[zl, yy] = obuf[s, zl]
        if s == 0:
            loads[9].wait()
        else:
            finish(s - 1, STEPS[s - 1])

    finish(3, STEPS[3])

    for s in range(4):
        for d in range(3):
            zi = (zl + d + 1) % 4
            copy(obuf.at[s, zi], orecv.at[zl, y], OUT + 3 * s + d, line[d]).wait_send()
        copy(send_core.at[s], got_core.at[s], CORE + s, sib).wait_send()
    for step in range(1, 5):
        for up, c in ring_pieces(step):
            ring(step, ring_from(step - 1, up), up, c).wait_send()
    for c in range(2):
        for n in range(2):
            for cp in [mate_a(n, c), opp_mate(n, c)] + y_copies(n, 0, c) + y_copies(n, 1, c):
                cp.wait_send()

    @pl.when(source)
    def _():
        for c in range(2):
            for n in range(2):
                for cp in [opp_y(n, c), opp_far(n, c)] + ([] if (n, c) == (1, 1) else [far_a(n, c)]):
                    cp.wait_send()
        cross(1).wait_send()

    @pl.when(jnp.logical_not(source))
    def _():
        cross(0).wait_send()
        to_relay.wait_send()
        far_a(1, 1).wait_send()


def exchange(*args):
    vm = pl.BlockSpec(memory_space=pltpu.VMEM)
    return pl.pallas_call(
        kernel,
        out_shape=jax.ShapeDtypeStruct((12, 192, 128), BF),
        in_specs=[pl.BlockSpec(memory_space=pltpu.HBM)] * len(args),
        out_specs=vm,
        scratch_shapes=[
            pltpu.VMEM((BLOCK, 256), BF),
            pltpu.VMEM((BLOCK, 256), BF),
            pltpu.VMEM((8, BLOCK, 256), BF),
            pltpu.VMEM((2, 32, 64, 256), BF),
            pltpu.VMEM((2, 64, 256), BF),
            pltpu.VMEM((2, 512, 128), F32),
            pltpu.VMEM((2, 2, 4, BLOCK, 256), BF),
            pltpu.VMEM((256, 512), BF),
            pltpu.VMEM((2, 6, 512, 256), BF),
            pltpu.VMEM((4, 2, 16, 128), F32),
            pltpu.VMEM((4, 2, 16, 128), F32),
            pltpu.VMEM((16, 128), F32),
            pltpu.VMEM((576, 128), F32),
            pltpu.VMEM((4, 576, 128), F32),
            pltpu.VMEM((4, 576, 128), F32),
            pltpu.VMEM((4, 4, 144, 128), BF),
            pltpu.VMEM((4, 4, 144, 128), BF),
            pltpu.VMEM((64, 64), BF),
            pltpu.VMEM((12, 192, 128), BF),
            pltpu.VMEM((HALVES[1][1], 256), BF),
            *[pltpu.VMEM(v.shape, v.dtype) for v in args[:9]],
            pltpu.SemaphoreType.DMA((N_SEMS,)),
            pltpu.SemaphoreType.DMA((N_SEMS,)),
            pltpu.SemaphoreType.DMA((10,)),
        ],
        compiler_params=pltpu.CompilerParams(
            collective_id=0, has_side_effects=True, vmem_limit_bytes=63 * 2**20
        ),
        name="outer_mean",
    )(*args)


def body(msa, flags, scale, shift, w_left, b_left, w_right, b_right, readout, pair):
    return exchange(
        msa.transpose(1, 2, 0), flags.T, scale[None], shift[None], w_left.T, b_left[None], w_right.T, b_right[None],
        readout, pair,
    )


def solution(mesh):
    in_specs = (
        P("seq", "res", None),
        P("seq", "res"),
        P(),
        P(),
        P(),
        P(),
        P(),
        P(),
        P(),
        P("res", "seq", None),
    )
    return jax.shard_map(
        body, mesh=mesh, in_specs=in_specs, out_specs=P("res", "seq", None), check_vma=False
    )
```

```python
import functools

import jax
import jax.numpy as jnp
from jax import lax
from jax.experimental import pallas as pl
from jax.experimental.pallas import tpu as pltpu
from jax.sharding import PartitionSpec as P

MESH = pl.DeviceIdType.MESH
NT = (((1,), (1,)), ((), ()))
BF, F32 = jnp.bfloat16, jnp.float32

RING_UP, RING_DOWN, PLANE = 0, 7, 14
FAR, MATE, Y_UP_A, Y_DN_A, Y_UP_B, Y_DN_B, OPP, MATE_OPP = range(8)
CROSS, CORE, COUNT, OUT = 46, 48, 52, 56
RELAY = 68
N_SEMS = 69
STEPS = (0, 3, 1, 2)
BLOCK = 400
HALVES = ((0, 208), (208, 192))


def place(x, y, z, k):
    return ((z // 4) * 2 + k, (x * 4 + y) * 4 + z % 4)


def kernel(
    msa_in, flags_in, scale_in, shift_in, w_left_in, b_left_in, w_right_in, b_right_in, readout_in, pair, out,
    lown, rown, lp, lc, lf, wide, rb, w2, xs, cnt, got_cnt, rcs, stage, send_core, got_core, obuf, orecv,
    w12, pairs, relay, msa, flags, scale, shift, w_left, b_left, w_right, b_right, readout, ssem, rsem, lsem,
):
    seq, res = lax.axis_index("seq"), lax.axis_index("res")
    h, k = seq // 2, seq % 2
    x, y, zl = res // 16, (res // 4) % 4, res % 4
    z = h * 4 + zl
    up_z, dn_z = place(x, y, (z + 1) % 8, k), place(x, y, (z + 7) % 8, k)
    anti, sib = place(x, y, (z + 4) % 8, k), place(x, y, z, 1 - k)
    up_y, dn_y = place(x, (y + 1) % 4, z, k), place(x, (y + 3) % 4, z, k)
    odd = x % 2
    mate = place((x + 1 + 2 * odd) % 4, y, z, k)
    far = place((x + 3 + 2 * odd) % 4, y, z, k)
    line = [place(x, y, h * 4 + (zl + d) % 4, k) for d in (1, 2, 3)]
    p = (x - 2 * h + 4) % 4
    source = p < 2
    a = ((p + 1) // 2) % 2
    b = 1 - a

    def copy(src, dst, sem, dev):
        return pltpu.make_async_remote_copy(
            src_ref=src,
            dst_ref=dst,
            send_sem=ssem.at[sem],
            recv_sem=rsem.at[sem],
            device_id=dev,
            device_id_type=MESH,
        )

    def same(ref, sem, dev):
        return copy(ref, ref, sem, dev)

    barrier = pltpu.get_barrier_semaphore()
    partners = [up_z, dn_z, anti, sib, up_y, dn_y, mate, far] + line
    for dev in partners:
        pl.semaphore_signal(barrier, inc=1, device_id=dev, device_id_type=MESH)

    loads = [
        pltpu.make_async_copy(src, dst, lsem.at[i])
        for i, (src, dst) in enumerate((
            (msa_in, msa), (flags_in, flags), (scale_in, scale), (shift_in, shift), (w_left_in, w_left),
            (b_left_in, b_left), (w_right_in, w_right), (b_right_in, b_right), (readout_in, readout), (pair, pairs),
        ))
    ]
    for load in loads:
        load.start()
    for load in loads[:8]:
        load.wait()
    w12[0:32, :] = w_left[...]
    w12[32:64, :] = w_right[...]

    def column(row):
        square = (row.shape[1], row.shape[1])
        diagonal = lax.broadcasted_iota(jnp.int32, square, 0) == lax.broadcasted_iota(jnp.int32, square, 1)
        return jnp.sum(jnp.where(diagonal, row, 0.0), axis=1, keepdims=True)

    gain, bias = column(scale[...]), column(shift[...])
    offset = jnp.concatenate([column(b_left[...]), column(b_right[...])], axis=0)

    def residue(i, carry):
        v = msa[i].astype(F32)
        c = v - jnp.mean(v, axis=0, keepdims=True)
        var = jnp.mean(c * c, axis=0, keepdims=True)
        normed = (c * lax.rsqrt(var + 1e-05) * gain + bias).astype(BF)
        both = jnp.dot(w12[...], normed, preferred_element_type=F32)
        both = ((both + offset) * flags[pl.ds(i, 1), :].astype(F32)).astype(BF)
        rows = pl.ds(pl.multiple_of(i * 32, 32), 32)
        lown[rows, :] = both[:32]
        rown[rows, :] = both[32:]
        return carry

    lax.fori_loop(0, 12, residue, 0, unroll=6)
    mask = jnp.concatenate([flags[...].astype(F32), jnp.zeros((4, 256), F32)], axis=0).astype(BF)
    lown[384:400, :] = mask
    rown[384:400, :] = mask
    wide[:, 384:512, :] = jnp.zeros((2, 128, 128), F32)
    pl.semaphore_wait(barrier, len(partners))

    def ring(step, zz, up, c):
        sem = (RING_UP if up else RING_DOWN) + 2 * (step - 1) + (c if step < 4 else 0)
        dst = lp.at[zz, pl.ds(*HALVES[c]), :]
        src = lown.at[pl.ds(*HALVES[c]), :] if step == 1 else dst
        return copy(src, dst, sem, up_z if up else dn_z)

    def ring_pieces(step):
        return [(up, c) for c in range(2) for up in (True, False) if step < 4 or up == (c == 0)]

    def ring_from(step, up):
        return (z + 8 - step) % 8 if up else (z + step) % 8

    def ring_on(step, c):
        for up in (True, False):
            ring(step, ring_from(step, up), up, c).wait_recv()
            if (up, c) in ring_pieces(step + 1):
                ring(step + 1, ring_from(step, up), up, c).start()

    def repack(src, zz):
        part, at = (zz // 4 + h) % 2, pl.ds(pl.multiple_of((zz % 4) * 16, 16), 16)
        for half in range(2):
            lanes = slice(half * 128, half * 128 + 128)
            wide[half, 0:384, :] = src[0:384, lanes].astype(F32)
            for c in range(32):
                lc[part, c, at, lanes] = wide[half, pl.ds(c, 16, stride=32), :].astype(BF)
        lf[part, at, :] = src[384:400, :]

    def ring_repack(step):
        repack(lp.at[(z + 8 - step) % 8], (z + 8 - step) % 8)
        repack(lp.at[(z + step) % 8], (z + step) % 8)

    def right(n, what, which, yy, dev, c):
        ref = rb.at[n, which, yy % 4, pl.ds(*HALVES[c]), :]
        return same(ref, PLANE + 2 * (8 * n + what) + c, dev)

    def far_a(n, c):
        return right(n, FAR, a, y, far, c)

    def mate_a(n, c):
        return right(n, MATE, a, y, mate, c)

    def y_copies(n, which, c):
        u, d = (Y_UP_A, Y_DN_A) if which == 0 else (Y_UP_B, Y_DN_B)
        side = a if which == 0 else b
        return [right(n, u, side, y, up_y, c), right(n, d, side, y, dn_y, c)]

    def opp_y(n, c):
        if n == 0:
            return right(n, OPP, a, y + 3, up_y, c)
        return right(n, OPP, a, y + 1, dn_y, c)

    def opp_far(n, c):
        return right(n, OPP, a, y + 2, far, c)

    def opp_mate(n, c):
        return right(n, MATE_OPP, a, y + 2, mate, c)

    def wait(n, what, c):
        which, yy = {
            FAR: (a, y), MATE: (b, y), Y_UP_A: (a, y + 3), Y_DN_A: (a, y + 1), Y_UP_B: (b, y + 3),
            Y_DN_B: (b, y + 1), OPP: (a, y + 2), MATE_OPP: (b, y + 2),
        }[what]
        right(n, what, which, yy, sib, c).wait_recv()

    def start(copies):
        for cp in copies:
            cp.start()

    def on_far(n, c):
        wait(n, FAR, c)
        start([mate_a(n, c)] + y_copies(n, 0, c))

    def on_mate(n, c):
        wait(n, MATE, c)
        start(y_copies(n, 1, c))

    def on_side(n, c):
        wait(n, Y_UP_A if n == 0 else Y_DN_A, c)
        opp_y(n, c).start()

    def on_opp(n, c):
        wait(n, OPP, c)
        start([opp_far(n, c), opp_mate(n, c)])

    def on_opp_far(n, c):
        wait(n, OPP, c)
        opp_mate(n, c).start()

    def cross(c):
        if c == 0:
            return copy(rown.at[pl.ds(*HALVES[0]), :], rb.at[1, odd, y, pl.ds(*HALVES[0]), :], CROSS, anti)
        return copy(relay, rb.at[1, 1 - odd, y, pl.ds(*HALVES[1]), :], CROSS + 1, anti)

    to_relay = copy(rown.at[pl.ds(*HALVES[1]), :], relay, RELAY, far)

    def on_cross(c):
        cross(c).wait_recv()
        start([far_a(1, c), mate_a(1, c)] + y_copies(1, 0, c))

    def prepare():
        loads[8].wait()
        for cp in range(16):
            w2[:, cp * 32 : cp * 32 + 32] = jnp.concatenate(
                [readout[cp * 64 : cp * 64 + 32, :].T, readout[cp * 64 + 32 : cp * 64 + 64, :].T], axis=0
            )
        repack(lown, z)

    @pl.when(source)
    def _():
        rb[0, odd, y] = rown[...]
        for c in range(2):
            start([far_a(0, c), mate_a(0, c)] + y_copies(0, 0, c))
            start([ring(1, z, up, c) for up in (True, False)])
        prepare()
        to_relay.wait_recv()
        cross(1).start()
        for c in range(2):
            on_mate(0, c)
            on_side(0, c)
            ring_on(1, c)
        on_cross(0)
        on_opp(0, 0)
        ring_on(2, 0)
        ring_repack(1)
        on_far(1, 1)
        ring_on(2, 1)
        on_opp(0, 1)
        on_mate(1, 0)
        on_side(1, 0)
        ring_on(3, 0)
        on_mate(1, 1)
        on_side(1, 1)
        ring_repack(2)
        ring_on(3, 1)
        ring_repack(3)

    @pl.when(jnp.logical_not(source))
    def _():
        to_relay.start()
        start([ring(1, z, up, 0) for up in (True, False)])
        cross(0).start()
        start([ring(1, z, up, 1) for up in (True, False)])
        prepare()
        for c in range(2):
            on_far(0, c)
            ring_on(1, c)
        on_mate(0, 0)
        on_cross(1)
        on_mate(0, 1)
        ring_on(2, 0)
        on_far(1, 0)
        ring_repack(1)
        ring_on(2, 1)
        on_opp_far(0, 0)
        on_opp_far(0, 1)
        on_mate(1, 0)
        ring_on(3, 0)
        ring_repack(2)
        on_mate(1, 1)
        ring_on(3, 1)
        ring_repack(3)

    def late(c, follow):
        @pl.when(jnp.logical_not(source) if follow else source)
        def _():
            on_opp_far(1, c) if follow else on_opp(1, c)

    for up, c in ring_pieces(4):
        ring(4, (z + 4) % 8, up, c).wait_recv()
    late(0, False)
    repack(lp.at[(z + 4) % 8], (z + 4) % 8)

    low = lax.broadcasted_iota(jnp.int32, (128, 128), 1) < 64

    def counts(s, yy):
        for which in range(2):
            t = jnp.zeros((16, 128), F32)
            for part in range(2):
                two = jnp.concatenate([lf[part], lf[part]], axis=0)
                t += lax.dot_general(
                    rb[part, which, yy, 384:400, :], two, NT, preferred_element_type=F32
                )
            cnt[s, which] = t

    def sides(yy):
        return [
            jnp.concatenate([rb[part, 0, yy, 0:384, :], rb[part, 1, yy, 0:384, :]], axis=0)
            for part in range(2)
        ]

    def tile(both, n):
        o = None
        for part in range(2):
            lt = lc[part, pl.ds(n * 4, 4), :, :].reshape(256, 256)
            t = lax.dot_general(both[part], lt, NT, preferred_element_type=F32)
            o = t if o is None else o + t
        ob = o.astype(BF).reshape(2, 6, 2, 32, 256)
        for jj in range(2):
            for cl in range(2):
                rows = pl.ds(pl.multiple_of(n * 64 + cl * 32, 32), 32)
                xs[:, :, rows, jj * 128 : jj * 128 + 128] = ob[:, :, jj, :, cl * 128 : cl * 128 + 128]

    def pair(which, jp, dst, side):
        q = jnp.dot(w2[...], xs[which, jp], preferred_element_type=F32)
        for jj in range(2):
            j = 2 * jp + jj
            c = jnp.where(low, q[:128, jj * 128 : jj * 128 + 128], q[128:, jj * 128 : jj * 128 + 128])
            t = (c * rcs[side, pl.ds(j, 1), :]).T
            s = t[:64] + t[64:]
            for zi in range(4):
                dst[pl.ds(zi * 144 + j, 12, stride=12), :] = s[zi * 16 : zi * 16 + 12]

    def arrive(off):
        for c in range(2):
            for n in range(2):
                if off == 2:
                    wait(n, MATE_OPP, c)
                if off in (1, 3):
                    first, second = (Y_UP_A, Y_UP_B) if off == 3 else (Y_DN_A, Y_DN_B)
                    if n == (0 if off == 3 else 1):

                        @pl.when(jnp.logical_not(source))
                        def _():
                            wait(n, first, c)
                    else:
                        wait(n, first, c)
                    wait(n, second, c)

    def finish(s, off):
        yy = (y + off) % 4
        for d in range(3):
            zi = (zl + d + 1) % 4
            src = (zl + 3 - d) % 4
            copy(obuf.at[s, zi], orecv.at[src, yy], OUT + 3 * s + d, line[d]).wait_recv()
        got = [orecv[q, yy].astype(F32) for q in range(4)]
        at = pl.ds(pl.multiple_of(yy * 48, 16), 48)
        for i in range(12):
            new = jnp.concatenate([g[i * 12 : i * 12 + 12] for g in got], axis=0)
            out[i, at, :] = (pairs[i, at, :].astype(F32) + new).astype(BF)

    def swap(s):
        return copy(send_core.at[s], got_core.at[s], CORE + s, sib)

    def settle(s):
        yy = (y + STEPS[s]) % 4
        swap(s).wait_recv()
        obuf[s] = (stage[...] + got_core[s]).astype(BF).reshape(4, 144, 128)
        for d in range(3):
            zi = (zl + d + 1) % 4
            copy(obuf.at[s, zi], orecv.at[zl, yy], OUT + 3 * s + d, line[d]).start()
        orecv[zl, yy] = obuf[s, zl]

    def swap_counts(s):
        return copy(cnt.at[s], got_cnt.at[s], COUNT + s, sib)

    def begin(s):
        arrive(STEPS[s])
        counts(s, (y + STEPS[s]) % 4)
        swap_counts(s).start()

    def multiply(s):
        both = sides((y + STEPS[s]) % 4)

        def one(n, carry):
            tile(both, n)
            return carry

        lax.fori_loop(0, 8, one, 0, unroll=True)

    def project(s):
        swap_counts(s).wait()
        for side, which in ((0, 1 - k), (1, k)):
            rcs[side] = 1.0 / (0.001 + cnt[s, which] + got_cnt[s, which])

        def block(which, dst, side):
            def one(jp, carry):
                pair(which, jp, dst, side)
                return carry

            lax.fori_loop(0, 6, one, 0, unroll=True)

        block(1 - k, send_core.at[s], 0)
        swap(s).start()
        block(k, stage, 1)

    begin(0)
    for s in range(4):
        multiply(s)
        if s == 0:
            late(1, False)
        if s == 1:
            late(1, True)
        project(s)
        if s == 0:
            late(0, True)
        if s < 3:
            begin(s + 1)
        else:
            loads[9].wait()
            finish(0, STEPS[0])
            finish(1, STEPS[1])
        settle(s)
    finish(2, STEPS[2])
    finish(3, STEPS[3])

    for s in range(4):
        for d in range(3):
            zi = (zl + d + 1) % 4
            copy(obuf.at[s, zi], orecv.at[zl, y], OUT + 3 * s + d, line[d]).wait_send()
        swap(s).wait_send()
    for step in range(1, 5):
        for up, c in ring_pieces(step):
            ring(step, ring_from(step - 1, up), up, c).wait_send()
    for c in range(2):
        for n in range(2):
            for cp in [mate_a(n, c), opp_mate(n, c)] + y_copies(n, 0, c) + y_copies(n, 1, c):
                cp.wait_send()

    @pl.when(source)
    def _():
        for c in range(2):
            for n in range(2):
                for cp in [opp_y(n, c), opp_far(n, c)] + ([] if (n, c) == (1, 1) else [far_a(n, c)]):
                    cp.wait_send()
        cross(1).wait_send()

    @pl.when(jnp.logical_not(source))
    def _():
        cross(0).wait_send()
        to_relay.wait_send()
        far_a(1, 1).wait_send()


def exchange(*args):
    vm = pl.BlockSpec(memory_space=pltpu.VMEM)
    return pl.pallas_call(
        kernel,
        out_shape=jax.ShapeDtypeStruct((12, 192, 128), BF),
        in_specs=[pl.BlockSpec(memory_space=pltpu.HBM)] * len(args),
        out_specs=vm,
        scratch_shapes=[
            pltpu.VMEM((BLOCK, 256), BF),
            pltpu.VMEM((BLOCK, 256), BF),
            pltpu.VMEM((8, BLOCK, 256), BF),
            pltpu.VMEM((2, 32, 64, 256), BF),
            pltpu.VMEM((2, 64, 256), BF),
            pltpu.VMEM((2, 512, 128), F32),
            pltpu.VMEM((2, 2, 4, BLOCK, 256), BF),
            pltpu.VMEM((256, 512), BF),
            pltpu.VMEM((2, 6, 512, 256), BF),
            pltpu.VMEM((4, 2, 16, 128), F32),
            pltpu.VMEM((4, 2, 16, 128), F32),
            pltpu.VMEM((2, 16, 128), F32),
            pltpu.VMEM((576, 128), F32),
            pltpu.VMEM((4, 576, 128), F32),
            pltpu.VMEM((4, 576, 128), F32),
            pltpu.VMEM((4, 4, 144, 128), BF),
            pltpu.VMEM((4, 4, 144, 128), BF),
            pltpu.VMEM((64, 64), BF),
            pltpu.VMEM((12, 192, 128), BF),
            pltpu.VMEM((HALVES[1][1], 256), BF),
            *[pltpu.VMEM(v.shape, v.dtype) for v in args[:9]],
            pltpu.SemaphoreType.DMA((N_SEMS,)),
            pltpu.SemaphoreType.DMA((N_SEMS,)),
            pltpu.SemaphoreType.DMA((10,)),
        ],
        compiler_params=pltpu.CompilerParams(
            collective_id=0, has_side_effects=True, vmem_limit_bytes=50_000_000
        ),
        name="outer_mean",
    )(*args)


def body(msa, flags, scale, shift, w_left, b_left, w_right, b_right, readout, pair):
    args = (
        msa.transpose(1, 2, 0), flags.T, scale[None], shift[None], w_left.T, b_left[None], w_right.T, b_right[None],
        readout, pair,
    )
    return exchange(*[pltpu.with_memory_space_constraint(v, pltpu.HBM) for v in args])


def solution(mesh):
    in_specs = (
        P("seq", "res", None),
        P("seq", "res"),
        P(),
        P(),
        P(),
        P(),
        P(),
        P(),
        P(),
        P("res", "seq", None),
    )
    return jax.shard_map(
        body, mesh=mesh, in_specs=in_specs, out_specs=P("res", "seq", None), check_vma=False
    )
```

```python
import functools

import jax
import jax.numpy as jnp
from jax import lax
from jax.experimental import pallas as pl
from jax.experimental.pallas import tpu as pltpu
from jax.sharding import PartitionSpec as P

MESH = pl.DeviceIdType.MESH
NT = (((1,), (1,)), ((), ()))
BF, F32 = jnp.bfloat16, jnp.float32

RING_UP, RING_DOWN, PLANE = 0, 7, 14
FAR, MATE, Y_UP_A, Y_DN_A, Y_UP_B, Y_DN_B, OPP, MATE_OPP = range(8)
CROSS, CORE, COUNT, OUT = 46, 48, 52, 56
RELAY = 68
N_SEMS = 69
STEPS = (0, 3, 1, 2)
AHEAD = 2
BLOCK = 400
HALVES = ((0, 208), (208, 192))


def place(x, y, z, k):
    return ((z // 4) * 2 + k, (x * 4 + y) * 4 + z % 4)


def kernel(
    msa_in, flags_in, scale_in, shift_in, w_left_in, b_left_in, w_right_in, b_right_in, readout_in, pair, out,
    lown, rown, lp, lc, lf, wide, rb, w2, xs, acc, cnt, got_cnt, rcs, stage, send_core, got_core, obuf, orecv,
    w12, pairs, relay, msa, flags, scale, shift, w_left, b_left, w_right, b_right, readout, ssem, rsem, lsem,
):
    seq, res = lax.axis_index("seq"), lax.axis_index("res")
    h, k = seq // 2, seq % 2
    x, y, zl = res // 16, (res // 4) % 4, res % 4
    z = h * 4 + zl
    up_z, dn_z = place(x, y, (z + 1) % 8, k), place(x, y, (z + 7) % 8, k)
    anti, sib = place(x, y, (z + 4) % 8, k), place(x, y, z, 1 - k)
    up_y, dn_y = place(x, (y + 1) % 4, z, k), place(x, (y + 3) % 4, z, k)
    odd = x % 2
    mate = place((x + 1 + 2 * odd) % 4, y, z, k)
    far = place((x + 3 + 2 * odd) % 4, y, z, k)
    line = [place(x, y, h * 4 + (zl + d) % 4, k) for d in (1, 2, 3)]
    p = (x - 2 * h + 4) % 4
    source = p < 2
    a = ((p + 1) // 2) % 2
    b = 1 - a

    def copy(src, dst, sem, dev):
        return pltpu.make_async_remote_copy(
            src_ref=src,
            dst_ref=dst,
            send_sem=ssem.at[sem],
            recv_sem=rsem.at[sem],
            device_id=dev,
            device_id_type=MESH,
        )

    def same(ref, sem, dev):
        return copy(ref, ref, sem, dev)

    barrier = pltpu.get_barrier_semaphore()
    partners = [up_z, dn_z, anti, sib, up_y, dn_y, mate, far] + line
    for dev in partners:
        pl.semaphore_signal(barrier, inc=1, device_id=dev, device_id_type=MESH)

    loads = [
        pltpu.make_async_copy(src, dst, lsem.at[i])
        for i, (src, dst) in enumerate((
            (msa_in, msa), (flags_in, flags), (scale_in, scale), (shift_in, shift), (w_left_in, w_left),
            (b_left_in, b_left), (w_right_in, w_right), (b_right_in, b_right), (readout_in, readout), (pair, pairs),
        ))
    ]
    for load in loads:
        load.start()
    for load in loads[:8]:
        load.wait()
    w12[0:32, :] = w_left[...]
    w12[32:64, :] = w_right[...]

    def column(row):
        square = (row.shape[1], row.shape[1])
        diagonal = lax.broadcasted_iota(jnp.int32, square, 0) == lax.broadcasted_iota(jnp.int32, square, 1)
        return jnp.sum(jnp.where(diagonal, row, 0.0), axis=1, keepdims=True)

    gain, bias = column(scale[...]), column(shift[...])
    offset = jnp.concatenate([column(b_left[...]), column(b_right[...])], axis=0)

    def residue(i, carry):
        v = msa[i].astype(F32)
        c = v - jnp.mean(v, axis=0, keepdims=True)
        var = jnp.mean(c * c, axis=0, keepdims=True)
        normed = (c * lax.rsqrt(var + 1e-05) * gain + bias).astype(BF)
        both = jnp.dot(w12[...], normed, preferred_element_type=F32)
        both = ((both + offset) * flags[pl.ds(i, 1), :].astype(F32)).astype(BF)
        rows = pl.ds(pl.multiple_of(i * 32, 32), 32)
        lown[rows, :] = both[:32]
        rown[rows, :] = both[32:]
        return carry

    lax.fori_loop(0, 12, residue, 0, unroll=6)
    mask = jnp.concatenate([flags[...].astype(F32), jnp.zeros((4, 256), F32)], axis=0).astype(BF)
    lown[384:400, :] = mask
    rown[384:400, :] = mask
    wide[:, 384:512, :] = jnp.zeros((2, 128, 128), F32)
    pl.semaphore_wait(barrier, len(partners))

    def ring(step, zz, up, c):
        sem = (RING_UP if up else RING_DOWN) + 2 * (step - 1) + (c if step < 4 else 0)
        dst = lp.at[zz, pl.ds(*HALVES[c]), :]
        src = lown.at[pl.ds(*HALVES[c]), :] if step == 1 else dst
        return copy(src, dst, sem, up_z if up else dn_z)

    def ring_pieces(step):
        return [(up, c) for c in range(2) for up in (True, False) if step < 4 or up == (c == 0)]

    def ring_from(step, up):
        return (z + 8 - step) % 8 if up else (z + step) % 8

    def ring_on(step, c):
        for up in (True, False):
            ring(step, ring_from(step, up), up, c).wait_recv()
            if (up, c) in ring_pieces(step + 1):
                ring(step + 1, ring_from(step, up), up, c).start()

    def repack(src, zz):
        part, at = (zz // 4 + h) % 2, pl.ds(pl.multiple_of((zz % 4) * 16, 16), 16)
        for half in range(2):
            lanes = slice(half * 128, half * 128 + 128)
            wide[half, 0:384, :] = src[0:384, lanes].astype(F32)
            for c in range(32):
                lc[part, c, at, lanes] = wide[half, pl.ds(c, 16, stride=32), :].astype(BF)
        lf[part, at, :] = src[384:400, :]

    def ring_repack(step):
        repack(lp.at[(z + 8 - step) % 8], (z + 8 - step) % 8)
        repack(lp.at[(z + step) % 8], (z + step) % 8)

    def right(n, what, which, yy, dev, c):
        ref = rb.at[n, which, yy % 4, pl.ds(*HALVES[c]), :]
        return same(ref, PLANE + 2 * (8 * n + what) + c, dev)

    def far_a(n, c):
        return right(n, FAR, a, y, far, c)

    def mate_a(n, c):
        return right(n, MATE, a, y, mate, c)

    def y_copies(n, which, c):
        u, d = (Y_UP_A, Y_DN_A) if which == 0 else (Y_UP_B, Y_DN_B)
        side = a if which == 0 else b
        return [right(n, u, side, y, up_y, c), right(n, d, side, y, dn_y, c)]

    def opp_y(n, c):
        if n == 0:
            return right(n, OPP, a, y + 3, up_y, c)
        return right(n, OPP, a, y + 1, dn_y, c)

    def opp_far(n, c):
        return right(n, OPP, a, y + 2, far, c)

    def opp_mate(n, c):
        return right(n, MATE_OPP, a, y + 2, mate, c)

    def wait(n, what, c):
        which, yy = {
            FAR: (a, y), MATE: (b, y), Y_UP_A: (a, y + 3), Y_DN_A: (a, y + 1), Y_UP_B: (b, y + 3),
            Y_DN_B: (b, y + 1), OPP: (a, y + 2), MATE_OPP: (b, y + 2),
        }[what]
        right(n, what, which, yy, sib, c).wait_recv()

    def start(copies):
        for cp in copies:
            cp.start()

    def on_far(n, c):
        wait(n, FAR, c)
        start([mate_a(n, c)] + y_copies(n, 0, c))

    def on_mate(n, c):
        wait(n, MATE, c)
        start(y_copies(n, 1, c))

    def on_side(n, c):
        wait(n, Y_UP_A if n == 0 else Y_DN_A, c)
        opp_y(n, c).start()

    def on_opp(n, c):
        wait(n, OPP, c)
        start([opp_far(n, c), opp_mate(n, c)])

    def on_opp_far(n, c):
        wait(n, OPP, c)
        opp_mate(n, c).start()

    def cross(c):
        if c == 0:
            return copy(rown.at[pl.ds(*HALVES[0]), :], rb.at[1, odd, y, pl.ds(*HALVES[0]), :], CROSS, anti)
        return copy(relay, rb.at[1, 1 - odd, y, pl.ds(*HALVES[1]), :], CROSS + 1, anti)

    to_relay = copy(rown.at[pl.ds(*HALVES[1]), :], relay, RELAY, far)

    def on_cross(c):
        cross(c).wait_recv()
        start([far_a(1, c), mate_a(1, c)] + y_copies(1, 0, c))

    def prepare():
        loads[8].wait()
        for cp in range(16):
            w2[:, cp * 32 : cp * 32 + 32] = jnp.concatenate(
                [readout[cp * 64 : cp * 64 + 32, :].T, readout[cp * 64 + 32 : cp * 64 + 64, :].T], axis=0
            )
        repack(lown, z)

    @pl.when(source)
    def _():
        rb[0, odd, y] = rown[...]
        for c in range(2):
            start([far_a(0, c), mate_a(0, c)] + y_copies(0, 0, c))
            start([ring(1, z, up, c) for up in (True, False)])
        prepare()
        to_relay.wait_recv()
        cross(1).start()
        for c in range(2):
            on_mate(0, c)
            on_side(0, c)
            ring_on(1, c)
        on_cross(0)
        on_opp(0, 0)
        ring_on(2, 0)
        ring_repack(1)
        on_far(1, 1)
        ring_on(2, 1)
        on_opp(0, 1)
        on_mate(1, 0)
        on_side(1, 0)
        ring_on(3, 0)
        on_mate(1, 1)
        on_side(1, 1)
        ring_repack(2)
        ring_on(3, 1)
        ring_repack(3)

    @pl.when(jnp.logical_not(source))
    def _():
        to_relay.start()
        start([ring(1, z, up, 0) for up in (True, False)])
        cross(0).start()
        start([ring(1, z, up, 1) for up in (True, False)])
        prepare()
        for c in range(2):
            on_far(0, c)
            ring_on(1, c)
        on_mate(0, 0)
        on_cross(1)
        on_mate(0, 1)
        ring_on(2, 0)
        on_far(1, 0)
        ring_repack(1)
        ring_on(2, 1)
        on_opp_far(0, 0)
        on_opp_far(0, 1)
        on_mate(1, 0)
        ring_on(3, 0)
        ring_repack(2)
        on_mate(1, 1)
        ring_on(3, 1)
        ring_repack(3)

    def late(c, follow):
        @pl.when(jnp.logical_not(source) if follow else source)
        def _():
            on_opp_far(1, c) if follow else on_opp(1, c)


    low = lax.broadcasted_iota(jnp.int32, (128, 128), 1) < 64

    def counts(s, yy):
        for which in range(2):
            t = jnp.zeros((16, 128), F32)
            for part in range(2):
                two = jnp.concatenate([lf[part], lf[part]], axis=0)
                t += lax.dot_general(
                    rb[part, which, yy, 384:400, :], two, NT, preferred_element_type=F32
                )
            cnt[s, which] = t

    def sides(part, yy):
        return jnp.concatenate([rb[part, 0, yy, 0:384, :], rb[part, 1, yy, 0:384, :]], axis=0)

    def dot(side, part, n):
        lt = lc[part, pl.ds(n * 4, 4), :, :].reshape(256, 256)
        return lax.dot_general(side, lt, NT, preferred_element_type=F32)

    def keep(o, n, cols, s):
        ob = o.astype(BF).reshape(-1, 6, 2, 32, 256)
        for jj in range(2):
            for cl in range(2):
                rows = pl.ds(pl.multiple_of(n * 64 + cl * 32, 32), 32)
                xs[s % 2, cols, :, rows, jj * 128 : jj * 128 + 128] = ob[:, :, jj, :, cl * 128 : cl * 128 + 128]

    def loop(lo, hi, one):
        def step(n, carry):
            one(n)
            return carry

        lax.fori_loop(lo, hi, step, 0, unroll=True)

    def ahead(s):
        side = sides(0, (y + STEPS[s]) % 4)

        def one(n):
            acc[s, n] = dot(side, 0, n)

        loop(0, 8, one)

    def multiply(s, lo, hi):
        yy = (y + STEPS[s]) % 4
        other = sides(1, yy)
        if s < AHEAD:

            def one(n):
                keep(acc[s, n] + dot(other, 1, n), n, slice(0, 2), s)
        else:
            own = sides(0, yy)

            def one(n):
                keep(dot(own, 0, n) + dot(other, 1, n), n, slice(0, 2), s)

        loop(lo, hi, one)

    def multiply_one(s, which, lo, hi):
        yy = (y + STEPS[s]) % 4
        own, other = rb[0, which, yy, 0:384, :], rb[1, which, yy, 0:384, :]

        def one(n):
            keep(dot(own, 0, n) + dot(other, 1, n), n, pl.ds(which, 1), s)

        loop(lo, hi, one)

    def pair(which, jp, dst, side, s):
        q = jnp.dot(w2[...], xs[s % 2, which, jp], preferred_element_type=F32)
        for jj in range(2):
            j = 2 * jp + jj
            c = jnp.where(low, q[:128, jj * 128 : jj * 128 + 128], q[128:, jj * 128 : jj * 128 + 128])
            t = (c * rcs[side, pl.ds(j, 1), :]).T
            u = t[:64] + t[64:]
            for zi in range(4):
                dst[pl.ds(zi * 144 + j, 12, stride=12), :] = u[zi * 16 : zi * 16 + 12]

    def arrive(off):
        for c in range(2):
            for n in range(2):
                if off == 2:
                    wait(n, MATE_OPP, c)
                if off == 3 and n == 1:
                    wait(1, Y_UP_A, c)
                    wait(1, Y_UP_B, c)
                if off == 1:
                    if n == 1:

                        @pl.when(jnp.logical_not(source))
                        def _():
                            wait(1, Y_DN_A, c)
                    else:
                        wait(0, Y_DN_A, c)
                    wait(n, Y_DN_B, c)

    def finish(s, off):
        yy = (y + off) % 4
        for d in range(3):
            zi = (zl + d + 1) % 4
            src = (zl + 3 - d) % 4
            copy(obuf.at[s, zi], orecv.at[src, yy], OUT + 3 * s + d, line[d]).wait_recv()
        got = [orecv[q, yy].astype(F32) for q in range(4)]
        at = pl.ds(pl.multiple_of(yy * 48, 16), 48)
        for i in range(12):
            new = jnp.concatenate([g[i * 12 : i * 12 + 12] for g in got], axis=0)
            out[i, at, :] = (pairs[i, at, :].astype(F32) + new).astype(BF)

    def swap(s):
        return copy(send_core.at[s], got_core.at[s], CORE + s, sib)

    def settle(s):
        yy = (y + STEPS[s]) % 4
        swap(s).wait_recv()
        obuf[s] = (stage[...] + got_core[s]).astype(BF).reshape(4, 144, 128)
        for d in range(3):
            zi = (zl + d + 1) % 4
            copy(obuf.at[s, zi], orecv.at[zl, yy], OUT + 3 * s + d, line[d]).start()
        orecv[zl, yy] = obuf[s, zl]

    def swap_counts(s):
        return copy(cnt.at[s], got_cnt.at[s], COUNT + s, sib)

    def begin(s):
        arrive(STEPS[s])
        counts(s, (y + STEPS[s]) % 4)
        swap_counts(s).start()

    def scales(s):
        swap_counts(s).wait()
        for side, which in ((0, 1 - k), (1, k)):
            rcs[side] = 1.0 / (0.001 + cnt[s, which] + got_cnt[s, which])

    def project(s, side):
        which, dst = ((1 - k), send_core.at[s]) if side == 0 else (k, stage)

        def one(jp):
            pair(which, jp, dst, side, s)

        loop(0, 6, one)
        if side == 0:
            swap(s).start()

    for c in range(2):

        @pl.when(jnp.logical_not(source))
        def _():
            wait(0, Y_UP_A, c)

        wait(0, Y_UP_B, c)
    for s in range(AHEAD):
        ahead(s)
    for up, c in ring_pieces(4):
        ring(4, (z + 4) % 8, up, c).wait_recv()
    late(0, False)
    repack(lp.at[(z + 4) % 8], (z + 4) % 8)
    begin(0)
    begin(1)
    multiply(0, 0, 8)
    late(1, False)
    multiply(1, 0, 8)
    scales(0)
    project(0, 0)
    project(0, 1)
    late(0, True)
    begin(2)
    multiply(2, 0, 2)
    settle(0)
    late(1, True)
    multiply(2, 2, 8)
    scales(1)
    project(1, 0)
    project(1, 1)
    scales(2)
    project(2, 0)
    settle(1)
    project(2, 1)
    begin(3)
    multiply_one(3, 1 - k, 0, 3)
    settle(2)
    multiply_one(3, 1 - k, 3, 8)
    scales(3)
    project(3, 0)
    multiply_one(3, k, 0, 8)
    project(3, 1)
    loads[9].wait()
    finish(0, STEPS[0])
    finish(1, STEPS[1])
    settle(3)
    finish(2, STEPS[2])
    finish(3, STEPS[3])

    for s in range(4):
        for d in range(3):
            zi = (zl + d + 1) % 4
            copy(obuf.at[s, zi], orecv.at[zl, y], OUT + 3 * s + d, line[d]).wait_send()
        swap(s).wait_send()
    for step in range(1, 5):
        for up, c in ring_pieces(step):
            ring(step, ring_from(step - 1, up), up, c).wait_send()
    for c in range(2):
        for n in range(2):
            for cp in [mate_a(n, c), opp_mate(n, c)] + y_copies(n, 0, c) + y_copies(n, 1, c):
                cp.wait_send()

    @pl.when(source)
    def _():
        for c in range(2):
            for n in range(2):
                for cp in [opp_y(n, c), opp_far(n, c)] + ([] if (n, c) == (1, 1) else [far_a(n, c)]):
                    cp.wait_send()
        cross(1).wait_send()

    @pl.when(jnp.logical_not(source))
    def _():
        cross(0).wait_send()
        to_relay.wait_send()
        far_a(1, 1).wait_send()


def exchange(*args):
    vm = pl.BlockSpec(memory_space=pltpu.VMEM)
    return pl.pallas_call(
        kernel,
        out_shape=jax.ShapeDtypeStruct((12, 192, 128), BF),
        in_specs=[pl.BlockSpec(memory_space=pltpu.HBM)] * len(args),
        out_specs=vm,
        scratch_shapes=[
            pltpu.VMEM((BLOCK, 256), BF),
            pltpu.VMEM((BLOCK, 256), BF),
            pltpu.VMEM((8, BLOCK, 256), BF),
            pltpu.VMEM((2, 32, 64, 256), BF),
            pltpu.VMEM((2, 64, 256), BF),
            pltpu.VMEM((2, 512, 128), F32),
            pltpu.VMEM((2, 2, 4, BLOCK, 256), BF),
            pltpu.VMEM((256, 512), BF),
            pltpu.VMEM((2, 2, 6, 512, 256), BF),
            pltpu.VMEM((AHEAD, 8, 768, 256), F32),
            pltpu.VMEM((4, 2, 16, 128), F32),
            pltpu.VMEM((4, 2, 16, 128), F32),
            pltpu.VMEM((2, 16, 128), F32),
            pltpu.VMEM((576, 128), F32),
            pltpu.VMEM((4, 576, 128), F32),
            pltpu.VMEM((4, 576, 128), F32),
            pltpu.VMEM((4, 4, 144, 128), BF),
            pltpu.VMEM((4, 4, 144, 128), BF),
            pltpu.VMEM((64, 64), BF),
            pltpu.VMEM((12, 192, 128), BF),
            pltpu.VMEM((HALVES[1][1], 256), BF),
            *[pltpu.VMEM(v.shape, v.dtype) for v in args[:9]],
            pltpu.SemaphoreType.DMA((N_SEMS,)),
            pltpu.SemaphoreType.DMA((N_SEMS,)),
            pltpu.SemaphoreType.DMA((10,)),
        ],
        compiler_params=pltpu.CompilerParams(
            collective_id=0, has_side_effects=True, vmem_limit_bytes=50_000_000
        ),
        name="outer_mean",
    )(*args)


def body(msa, flags, scale, shift, w_left, b_left, w_right, b_right, readout, pair):
    args = (
        msa.transpose(1, 2, 0), flags.T, scale[None], shift[None], w_left.T, b_left[None], w_right.T, b_right[None],
        readout, pair,
    )
    return exchange(*[pltpu.with_memory_space_constraint(v, pltpu.HBM) for v in args])


def solution(mesh):
    in_specs = (
        P("seq", "res", None),
        P("seq", "res"),
        P(),
        P(),
        P(),
        P(),
        P(),
        P(),
        P(),
        P("res", "seq", None),
    )
    return jax.shard_map(
        body, mesh=mesh, in_specs=in_specs, out_specs=P("res", "seq", None), check_vma=False
    )
```

```python
import functools

import jax
import jax.numpy as jnp
from jax import lax
from jax.experimental import pallas as pl
from jax.experimental.pallas import tpu as pltpu
from jax.sharding import PartitionSpec as P

MESH = pl.DeviceIdType.MESH
NT = (((1,), (1,)), ((), ()))
BF, F32 = jnp.bfloat16, jnp.float32

RING_UP, RING_DOWN, PLANE = 0, 7, 14
FAR, MATE, Y_UP_A, Y_DN_A, Y_UP_B, Y_DN_B, OPP, MATE_OPP = range(8)
CROSS, CORE, COUNT, OUT = 46, 48, 52, 56
RELAY = 68
N_SEMS = 69
STEPS = (0, 3, 1, 2)
AHEAD = 2
BLOCK = 400
HALVES = ((0, 208), (208, 192))


def place(x, y, z, k):
    return ((z // 4) * 2 + k, (x * 4 + y) * 4 + z % 4)


def kernel(
    msa_in, flags_in, scale_in, shift_in, w_left_in, b_left_in, w_right_in, b_right_in, readout_in, pair, out,
    lown, rown, lp, lc, lf, wide, rb, w2, xs, acc, cnt, got_cnt, rcs, stage, send_core, got_core, obuf, orecv,
    w12, pairs, relay, msa, flags, scale, shift, w_left, b_left, w_right, b_right, readout, ssem, rsem, lsem,
):
    seq, res = lax.axis_index("seq"), lax.axis_index("res")
    h, k = seq // 2, seq % 2
    x, y, zl = res // 16, (res // 4) % 4, res % 4
    z = h * 4 + zl
    up_z, dn_z = place(x, y, (z + 1) % 8, k), place(x, y, (z + 7) % 8, k)
    anti, sib = place(x, y, (z + 4) % 8, k), place(x, y, z, 1 - k)
    up_y, dn_y = place(x, (y + 1) % 4, z, k), place(x, (y + 3) % 4, z, k)
    odd = x % 2
    mate = place((x + 1 + 2 * odd) % 4, y, z, k)
    far = place((x + 3 + 2 * odd) % 4, y, z, k)
    line = [place(x, y, h * 4 + (zl + d) % 4, k) for d in (1, 2, 3)]
    p = (x - 2 * h + 4) % 4
    source = p < 2
    a = ((p + 1) // 2) % 2
    b = 1 - a

    def copy(src, dst, sem, dev):
        return pltpu.make_async_remote_copy(
            src_ref=src,
            dst_ref=dst,
            send_sem=ssem.at[sem],
            recv_sem=rsem.at[sem],
            device_id=dev,
            device_id_type=MESH,
        )

    def same(ref, sem, dev):
        return copy(ref, ref, sem, dev)

    barrier = pltpu.get_barrier_semaphore()
    partners = [up_z, dn_z, anti, sib, up_y, dn_y, mate, far] + line
    for dev in partners:
        pl.semaphore_signal(barrier, inc=1, device_id=dev, device_id_type=MESH)

    loads = [
        pltpu.make_async_copy(src, dst, lsem.at[i])
        for i, (src, dst) in enumerate((
            (msa_in, msa), (flags_in, flags), (scale_in, scale), (shift_in, shift), (w_left_in, w_left),
            (b_left_in, b_left), (w_right_in, w_right), (b_right_in, b_right), (readout_in, readout), (pair, pairs),
        ))
    ]
    for load in loads:
        load.start()
    for load in loads[:8]:
        load.wait()
    w12[0:32, :] = w_left[...]
    w12[32:64, :] = w_right[...]

    def column(row):
        square = (row.shape[1], row.shape[1])
        diagonal = lax.broadcasted_iota(jnp.int32, square, 0) == lax.broadcasted_iota(jnp.int32, square, 1)
        return jnp.sum(jnp.where(diagonal, row, 0.0), axis=1, keepdims=True)

    gain, bias = column(scale[...]), column(shift[...])
    offset = jnp.concatenate([column(b_left[...]), column(b_right[...])], axis=0)

    def residue(i, carry):
        v = msa[i].astype(F32)
        c = v - jnp.mean(v, axis=0, keepdims=True)
        var = jnp.mean(c * c, axis=0, keepdims=True)
        normed = (c * lax.rsqrt(var + 1e-05) * gain + bias).astype(BF)
        both = jnp.dot(w12[...], normed, preferred_element_type=F32)
        both = ((both + offset) * flags[pl.ds(i, 1), :].astype(F32)).astype(BF)
        rows = pl.ds(pl.multiple_of(i * 32, 32), 32)
        lown[rows, :] = both[:32]
        rown[rows, :] = both[32:]
        return carry

    lax.fori_loop(0, 12, residue, 0, unroll=6)
    mask = jnp.concatenate([flags[...].astype(F32), jnp.zeros((4, 256), F32)], axis=0).astype(BF)
    lown[384:400, :] = mask
    rown[384:400, :] = mask
    wide[:, 384:512, :] = jnp.zeros((2, 128, 128), F32)
    pl.semaphore_wait(barrier, len(partners))

    def ring(step, zz, up, c):
        sem = (RING_UP if up else RING_DOWN) + 2 * (step - 1) + (c if step < 4 else 0)
        dst = lp.at[zz, pl.ds(*HALVES[c]), :]
        src = lown.at[pl.ds(*HALVES[c]), :] if step == 1 else dst
        return copy(src, dst, sem, up_z if up else dn_z)

    def ring_pieces(step):
        return [(up, c) for c in range(2) for up in (True, False) if step < 4 or up == (c == 0)]

    def ring_from(step, up):
        return (z + 8 - step) % 8 if up else (z + step) % 8

    def ring_on(step, c):
        for up in (True, False):
            ring(step, ring_from(step, up), up, c).wait_recv()
            if (up, c) in ring_pieces(step + 1):
                ring(step + 1, ring_from(step, up), up, c).start()

    def repack(src, zz):
        part, at = (zz // 4 + h) % 2, pl.ds(pl.multiple_of((zz % 4) * 16, 16), 16)
        for half in range(2):
            lanes = slice(half * 128, half * 128 + 128)
            wide[half, 0:384, :] = src[0:384, lanes].astype(F32)
            for c in range(32):
                lc[part, c, at, lanes] = wide[half, pl.ds(c, 16, stride=32), :].astype(BF)
        lf[part, at, :] = src[384:400, :]

    def ring_repack(step):
        repack(lp.at[(z + 8 - step) % 8], (z + 8 - step) % 8)
        repack(lp.at[(z + step) % 8], (z + step) % 8)

    def right(n, what, which, yy, dev, c):
        ref = rb.at[n, which, yy % 4, pl.ds(*HALVES[c]), :]
        return same(ref, PLANE + 2 * (8 * n + what) + c, dev)

    def far_a(n, c):
        return right(n, FAR, a, y, far, c)

    def mate_a(n, c):
        return right(n, MATE, a, y, mate, c)

    def y_copies(n, which, c):
        u, d = (Y_UP_A, Y_DN_A) if which == 0 else (Y_UP_B, Y_DN_B)
        side = a if which == 0 else b
        return [right(n, u, side, y, up_y, c), right(n, d, side, y, dn_y, c)]

    def opp_y(n, c):
        if n == 0:
            return right(n, OPP, a, y + 3, up_y, c)
        return right(n, OPP, a, y + 1, dn_y, c)

    def opp_far(n, c):
        return right(n, OPP, a, y + 2, far, c)

    def opp_mate(n, c):
        return right(n, MATE_OPP, a, y + 2, mate, c)

    def wait(n, what, c):
        which, yy = {
            FAR: (a, y), MATE: (b, y), Y_UP_A: (a, y + 3), Y_DN_A: (a, y + 1), Y_UP_B: (b, y + 3),
            Y_DN_B: (b, y + 1), OPP: (a, y + 2), MATE_OPP: (b, y + 2),
        }[what]
        right(n, what, which, yy, sib, c).wait_recv()

    def start(copies):
        for cp in copies:
            cp.start()

    def on_far(n, c):
        wait(n, FAR, c)
        start([mate_a(n, c)] + y_copies(n, 0, c))

    def on_mate(n, c):
        wait(n, MATE, c)
        start(y_copies(n, 1, c))

    def on_side(n, c):
        wait(n, Y_UP_A if n == 0 else Y_DN_A, c)
        opp_y(n, c).start()

    def on_opp(n, c):
        wait(n, OPP, c)
        start([opp_far(n, c), opp_mate(n, c)])

    def on_opp_far(n, c):
        wait(n, OPP, c)
        opp_mate(n, c).start()

    def cross(c):
        if c == 0:
            return copy(rown.at[pl.ds(*HALVES[0]), :], rb.at[1, odd, y, pl.ds(*HALVES[0]), :], CROSS, anti)
        return copy(relay, rb.at[1, 1 - odd, y, pl.ds(*HALVES[1]), :], CROSS + 1, anti)

    to_relay = copy(rown.at[pl.ds(*HALVES[1]), :], relay, RELAY, far)

    def on_cross(c):
        cross(c).wait_recv()
        start([far_a(1, c), mate_a(1, c)] + y_copies(1, 0, c))

    def prepare():
        loads[8].wait()
        for cp in range(16):
            w2[:, cp * 32 : cp * 32 + 32] = jnp.concatenate(
                [readout[cp * 64 : cp * 64 + 32, :].T, readout[cp * 64 + 32 : cp * 64 + 64, :].T], axis=0
            )
        repack(lown, z)

    @pl.when(source)
    def _():
        rb[0, odd, y] = rown[...]
        for c in range(2):
            start([far_a(0, c), mate_a(0, c)] + y_copies(0, 0, c))
            start([ring(1, z, up, c) for up in (True, False)])
        prepare()
        to_relay.wait_recv()
        cross(1).start()
        for c in range(2):
            on_mate(0, c)
            on_side(0, c)
            ring_on(1, c)
        on_cross(0)
        ring_on(2, 0)
        ring_repack(1)
        on_far(1, 1)
        ring_on(2, 1)
        on_mate(1, 0)
        on_side(1, 0)
        ring_on(3, 0)
        on_opp(0, 0)
        on_opp(0, 1)
        on_mate(1, 1)
        on_side(1, 1)
        ring_repack(2)
        ring_on(3, 1)
        ring_repack(3)

    @pl.when(jnp.logical_not(source))
    def _():
        to_relay.start()
        start([ring(1, z, up, 0) for up in (True, False)])
        cross(0).start()
        start([ring(1, z, up, 1) for up in (True, False)])
        prepare()
        for c in range(2):
            on_far(0, c)
            ring_on(1, c)
        on_mate(0, 0)
        on_cross(1)
        on_mate(0, 1)
        ring_on(2, 0)
        on_far(1, 0)
        ring_repack(1)
        ring_on(2, 1)
        on_mate(1, 0)
        ring_on(3, 0)
        ring_repack(2)
        on_mate(1, 1)
        ring_on(3, 1)
        on_opp_far(0, 0)
        on_opp_far(0, 1)
        ring_repack(3)

    def late(c, follow):
        @pl.when(jnp.logical_not(source) if follow else source)
        def _():
            on_opp_far(1, c) if follow else on_opp(1, c)


    low = lax.broadcasted_iota(jnp.int32, (128, 128), 1) < 64

    def counts(s, yy):
        for which in range(2):
            t = jnp.zeros((16, 128), F32)
            for part in range(2):
                two = jnp.concatenate([lf[part], lf[part]], axis=0)
                t += lax.dot_general(
                    rb[part, which, yy, 384:400, :], two, NT, preferred_element_type=F32
                )
            cnt[s, which] = t

    def sides(part, yy):
        return jnp.concatenate([rb[part, 0, yy, 0:384, :], rb[part, 1, yy, 0:384, :]], axis=0)

    def dot(side, part, n):
        lt = lc[part, pl.ds(n * 4, 4), :, :].reshape(256, 256)
        return lax.dot_general(side, lt, NT, preferred_element_type=F32)

    def keep(o, n, cols, s):
        ob = o.astype(BF).reshape(-1, 6, 2, 32, 256)
        for jj in range(2):
            for cl in range(2):
                rows = pl.ds(pl.multiple_of(n * 64 + cl * 32, 32), 32)
                xs[s % 2, cols, :, rows, jj * 128 : jj * 128 + 128] = ob[:, :, jj, :, cl * 128 : cl * 128 + 128]

    def loop(lo, hi, one):
        def step(n, carry):
            one(n)
            return carry

        lax.fori_loop(lo, hi, step, 0, unroll=True)

    def ahead(s):
        side = sides(0, (y + STEPS[s]) % 4)

        def one(n):
            acc[s, n] = dot(side, 0, n)

        loop(0, 8, one)

    def multiply(s, lo, hi):
        yy = (y + STEPS[s]) % 4
        other = sides(1, yy)
        if s < AHEAD:

            def one(n):
                keep(acc[s, n] + dot(other, 1, n), n, slice(0, 2), s)
        else:
            own = sides(0, yy)

            def one(n):
                keep(dot(own, 0, n) + dot(other, 1, n), n, slice(0, 2), s)

        loop(lo, hi, one)

    def multiply_one(s, which, lo, hi):
        yy = (y + STEPS[s]) % 4
        own, other = rb[0, which, yy, 0:384, :], rb[1, which, yy, 0:384, :]

        def one(n):
            keep(dot(own, 0, n) + dot(other, 1, n), n, pl.ds(which, 1), s)

        loop(lo, hi, one)

    def pair(which, jp, dst, side, s):
        q = jnp.dot(w2[...], xs[s % 2, which, jp], preferred_element_type=F32)
        for jj in range(2):
            j = 2 * jp + jj
            c = jnp.where(low, q[:128, jj * 128 : jj * 128 + 128], q[128:, jj * 128 : jj * 128 + 128])
            t = (c * rcs[side, pl.ds(j, 1), :]).T
            u = t[:64] + t[64:]
            for zi in range(4):
                dst[pl.ds(zi * 144 + j, 12, stride=12), :] = u[zi * 16 : zi * 16 + 12]

    def arrive(off):
        for c in range(2):
            for n in range(2):
                if off == 2:
                    wait(n, MATE_OPP, c)
                if off == 3 and n == 1:
                    wait(1, Y_UP_A, c)
                    wait(1, Y_UP_B, c)
                if off == 1:
                    if n == 1:

                        @pl.when(jnp.logical_not(source))
                        def _():
                            wait(1, Y_DN_A, c)
                    else:
                        wait(0, Y_DN_A, c)
                    wait(n, Y_DN_B, c)

    def finish(s, off):
        yy = (y + off) % 4
        for d in range(3):
            zi = (zl + d + 1) % 4
            src = (zl + 3 - d) % 4
            copy(obuf.at[s, zi], orecv.at[src, yy], OUT + 3 * s + d, line[d]).wait_recv()
        got = [orecv[q, yy].astype(F32) for q in range(4)]
        at = pl.ds(pl.multiple_of(yy * 48, 16), 48)
        for i in range(12):
            new = jnp.concatenate([g[i * 12 : i * 12 + 12] for g in got], axis=0)
            out[i, at, :] = (pairs[i, at, :].astype(F32) + new).astype(BF)

    def swap(s):
        return copy(send_core.at[s], got_core.at[s], CORE + s, sib)

    def settle(s):
        yy = (y + STEPS[s]) % 4
        swap(s).wait_recv()
        obuf[s] = (stage[...] + got_core[s]).astype(BF).reshape(4, 144, 128)
        for d in range(3):
            zi = (zl + d + 1) % 4
            copy(obuf.at[s, zi], orecv.at[zl, yy], OUT + 3 * s + d, line[d]).start()
        orecv[zl, yy] = obuf[s, zl]

    def swap_counts(s):
        return copy(cnt.at[s], got_cnt.at[s], COUNT + s, sib)

    def begin(s):
        arrive(STEPS[s])
        counts(s, (y + STEPS[s]) % 4)
        swap_counts(s).start()

    def scales(s):
        swap_counts(s).wait()
        for side, which in ((0, 1 - k), (1, k)):
            rcs[side] = 1.0 / (0.001 + cnt[s, which] + got_cnt[s, which])

    def project(s, side):
        which, dst = ((1 - k), send_core.at[s]) if side == 0 else (k, stage)

        def one(jp):
            pair(which, jp, dst, side, s)

        loop(0, 6, one)
        if side == 0:
            swap(s).start()

    for c in range(2):

        @pl.when(jnp.logical_not(source))
        def _():
            wait(0, Y_UP_A, c)

        wait(0, Y_UP_B, c)
    for s in range(AHEAD):
        ahead(s)
    for up, c in ring_pieces(4):
        ring(4, (z + 4) % 8, up, c).wait_recv()
    late(0, False)
    repack(lp.at[(z + 4) % 8], (z + 4) % 8)
    begin(0)
    begin(1)
    multiply(0, 0, 8)
    late(1, False)
    multiply(1, 0, 8)
    scales(0)
    project(0, 0)
    project(0, 1)
    late(0, True)
    begin(2)
    multiply(2, 0, 2)
    settle(0)
    late(1, True)
    multiply(2, 2, 8)
    scales(1)
    project(1, 0)
    project(1, 1)
    scales(2)
    project(2, 0)
    settle(1)
    project(2, 1)
    begin(3)
    multiply_one(3, 1 - k, 0, 3)
    settle(2)
    multiply_one(3, 1 - k, 3, 8)
    scales(3)
    project(3, 0)
    multiply_one(3, k, 0, 8)
    project(3, 1)
    loads[9].wait()
    finish(0, STEPS[0])
    finish(1, STEPS[1])
    settle(3)
    finish(2, STEPS[2])
    finish(3, STEPS[3])

    for s in range(4):
        for d in range(3):
            zi = (zl + d + 1) % 4
            copy(obuf.at[s, zi], orecv.at[zl, y], OUT + 3 * s + d, line[d]).wait_send()
        swap(s).wait_send()
    for step in range(1, 5):
        for up, c in ring_pieces(step):
            ring(step, ring_from(step - 1, up), up, c).wait_send()
    for c in range(2):
        for n in range(2):
            for cp in [mate_a(n, c), opp_mate(n, c)] + y_copies(n, 0, c) + y_copies(n, 1, c):
                cp.wait_send()

    @pl.when(source)
    def _():
        for c in range(2):
            for n in range(2):
                for cp in [opp_y(n, c), opp_far(n, c)] + ([] if (n, c) == (1, 1) else [far_a(n, c)]):
                    cp.wait_send()
        cross(1).wait_send()

    @pl.when(jnp.logical_not(source))
    def _():
        cross(0).wait_send()
        to_relay.wait_send()
        far_a(1, 1).wait_send()


def exchange(*args):
    vm = pl.BlockSpec(memory_space=pltpu.VMEM)
    return pl.pallas_call(
        kernel,
        out_shape=jax.ShapeDtypeStruct((12, 192, 128), BF),
        in_specs=[pl.BlockSpec(memory_space=pltpu.HBM)] * len(args),
        out_specs=vm,
        scratch_shapes=[
            pltpu.VMEM((BLOCK, 256), BF),
            pltpu.VMEM((BLOCK, 256), BF),
            pltpu.VMEM((8, BLOCK, 256), BF),
            pltpu.VMEM((2, 32, 64, 256), BF),
            pltpu.VMEM((2, 64, 256), BF),
            pltpu.VMEM((2, 512, 128), F32),
            pltpu.VMEM((2, 2, 4, BLOCK, 256), BF),
            pltpu.VMEM((256, 512), BF),
            pltpu.VMEM((2, 2, 6, 512, 256), BF),
            pltpu.VMEM((AHEAD, 8, 768, 256), F32),
            pltpu.VMEM((4, 2, 16, 128), F32),
            pltpu.VMEM((4, 2, 16, 128), F32),
            pltpu.VMEM((2, 16, 128), F32),
            pltpu.VMEM((576, 128), F32),
            pltpu.VMEM((4, 576, 128), F32),
            pltpu.VMEM((4, 576, 128), F32),
            pltpu.VMEM((4, 4, 144, 128), BF),
            pltpu.VMEM((4, 4, 144, 128), BF),
            pltpu.VMEM((64, 64), BF),
            pltpu.VMEM((12, 192, 128), BF),
            pltpu.VMEM((HALVES[1][1], 256), BF),
            *[pltpu.VMEM(v.shape, v.dtype) for v in args[:9]],
            pltpu.SemaphoreType.DMA((N_SEMS,)),
            pltpu.SemaphoreType.DMA((N_SEMS,)),
            pltpu.SemaphoreType.DMA((10,)),
        ],
        compiler_params=pltpu.CompilerParams(
            collective_id=0, has_side_effects=True, vmem_limit_bytes=50_000_000
        ),
        name="outer_mean",
    )(*args)


def body(msa, flags, scale, shift, w_left, b_left, w_right, b_right, readout, pair):
    args = (
        msa.transpose(1, 2, 0), flags.T, scale[None], shift[None], w_left.T, b_left[None], w_right.T, b_right[None],
        readout, pair,
    )
    return exchange(*[pltpu.with_memory_space_constraint(v, pltpu.HBM) for v in args])


def solution(mesh):
    in_specs = (
        P("seq", "res", None),
        P("seq", "res"),
        P(),
        P(),
        P(),
        P(),
        P(),
        P(),
        P(),
        P("res", "seq", None),
    )
    return jax.shard_map(
        body, mesh=mesh, in_specs=in_specs, out_specs=P("res", "seq", None), check_vma=False
    )
```
